32 devices in a mesh: depth: 16 (over z, x, core), az: 2 (over y).
Axes of the slice: x: 2, y: 2, z: 4, core: 2. Of those that a mesh axis runs over, the one named last changes fastest.
Arguments:
- velocity: float32 [6, 256, 64, 128], P(None, 'depth', 'az'), may hold values from -6 to 6
- stress: float32 [7, 256, 64, 128], P(None, 'depth', 'az'), may hold values from -6 to 6
- memory: float32 [12, 256, 64, 128], P(None, 'depth', 'az'), may hold values from -3 to 3
- layer_ids: int32 [64, 32], P('depth'), may hold values from 0 to 7, as said below
- materials: float32 [8, 8], replicated, may hold values from 0.006 to 4, as said below
- jkd: float32 [8, 9], replicated, may hold values from 0.1 to 60, as said below
- source_depth: int32 [1], replicated, may hold values from 0 to 255
Outputs:
- velocity_out: float32 [6, 256, 64, 128], P(None, 'depth', 'az')
- stress_out: float32 [7, 256, 64, 128], P(None, 'depth', 'az')
- memory_out: float32 [12, 256, 64, 128], P(None, 'depth', 'az')
The draws below stay inside these ranges and needn't reach their ends.
Inputs may be any that keep to these rules, and one draw needn't show every extreme that they name: `layer_ids`: the first 4 radial elements hold 0 (borehole fluid); beyond them each depth element holds one formation row of 1 to 7 for all its radial elements. `materials`: columns: lambda0 0.5 to 1.5, shear modulus 0.3 to 1 (row 0: 0.006 to 0.02), M 0.5 to 1.5, beta 0.3 to 0.9, bulk density 1.5 to 2.5, fluid density 0.8 to 1.2, tortuosity 1.5 to 4, friction 0.5 to 2. `jkd`: omega 0.5 to 5, pole weights 0.1 to 1, pole rates 0.3 to 60.
All inputs are finite; a program needn't handle non-finite values.
Results may differ from the reference program's by a relative error of at most 0.0001.
Values sent between devices are 32-bit elements; how exact they have to be, the bound alone decides.
A program may use at most 128 MiB of HBM per device.

```python
import math
import jax
import jax.numpy as jnp
import numpy as np
from jax import lax

NR = 128
NT = 64
STEPS = 2
NMAT = 8
RB = 4
NZ = 256


def draw_layer_ids(key, part):
    layers = jax.random.randint(key, (NZ // 4, 1), 1, NMAT)
    radial_index = jnp.arange(NR // 4)[None, :]
    return jnp.where(radial_index < RB, 0, layers).astype(jnp.int32)


def draw_materials(key, part):
    unit_draw = jax.random.uniform(key, (NMAT, 8), jnp.float32)
    lower_end = jnp.array([0.5, 0.3, 0.5, 0.3, 1.5, 0.8, 1.5, 0.5], jnp.float32)
    upper_end = jnp.array([1.5, 1.0, 1.5, 0.9, 2.5, 1.2, 4.0, 2.0], jnp.float32)
    values = lower_end + (upper_end - lower_end) * unit_draw
    fluid_cell = (jnp.arange(NMAT) == 0)[:, None] & (jnp.arange(8) == 1)[None, :]
    return jnp.where(fluid_cell, 0.02 * values, values).astype(jnp.float32)


def draw_jkd(key, part):
    unit_draw = jax.random.uniform(key, (NMAT, 9), jnp.float32)
    column = jnp.arange(9)[None, :]
    omega_part = 0.5 + 4.5 * unit_draw
    weight_part = 0.1 + 0.9 * unit_draw
    rate_part = jnp.exp(math.log(0.3) + (math.log(60.0) - math.log(0.3)) * unit_draw)
    return jnp.where(column == 0, omega_part, jnp.where(column < 5, weight_part, rate_part)).astype(jnp.float32)


def levels(rng, extent, pieces, low, high):
    gain = 1.0
    for dim, blocks in pieces:
        heights = jax.random.uniform(jax.random.fold_in(jax.random.fold_in(rng, 6), dim), (blocks,), jnp.float32, low / len(pieces), high / len(pieces))
        gain = gain * jnp.repeat(jnp.exp(heights), extent[dim] // blocks).reshape((-1,) + (1,) * (len(extent) - 1 - dim))
    return gain


def noise(rng, dims, deviation, reach, shards=(), kind=jnp.bfloat16):
    loudness = levels(rng, dims, shards, -0.22, 0.18) if shards else 1.0
    entries = jax.random.normal(rng, dims, jnp.float32) * deviation * loudness
    return jnp.minimum(jnp.maximum(entries, -reach), reach).astype(kind)


def setup_inputs(seed: int = 0) -> dict:
    arg_keys = jax.random.split(jax.random.key(seed), 8)
    return {
        "velocity": noise(arg_keys[0], (6, NZ, NT, NR), 1.0, 6.0, ((1, 16), (2, 2)), jnp.float32),
        "stress": noise(arg_keys[1], (7, NZ, NT, NR), 1.0, 6.0, ((1, 16), (2, 2)), jnp.float32),
        "memory": noise(arg_keys[2], (12, NZ, NT, NR), 0.5, 3.0, ((1, 16), (2, 2)), jnp.float32),
        "layer_ids": draw_layer_ids(jax.random.fold_in(arg_keys[7], 71), 0),
        "materials": draw_materials(jax.random.fold_in(arg_keys[7], 71), 0),
        "jkd": draw_jkd(jax.random.fold_in(arg_keys[7], 71), 0),
        "source_depth": jax.random.randint(arg_keys[6], (1,), 0, NZ).astype(jnp.int32),
    }


DT = 0.02
SOURCE_GAIN = 40.0
R_INNER = 1.0
HIGHEST = lax.Precision.HIGHEST

def gll_basis():
    root_value = math.sqrt(3.0 / 7.0)
    gll_nodes = np.array([-1.0, -root_value, 0.0, root_value, 1.0])
    weights = np.array([0.1, 49.0 / 90.0, 32.0 / 45.0, 49.0 / 90.0, 0.1])
    offsets = gll_nodes[:, None] - gll_nodes[None, :] + np.eye(5)
    factors = np.prod(offsets, axis=1)
    derivative = factors[:, None] / factors[None, :] / offsets
    diagonal_part = np.sum(1.0 / offsets, axis=1) - 1.0
    derivative = derivative * (1.0 - np.eye(5)) + np.eye(5) * diagonal_part[:, None]
    return (gll_nodes, weights, derivative)

def radial_operator(node_count):
    gll_nodes, weights, derivative = gll_basis()
    full_count = node_count + 1
    stencil = weights[:, None] * derivative * 2.0
    assembled = np.zeros((full_count, full_count))
    node_mass = np.zeros(full_count)
    for element in range(node_count // 4):
        assembled[4 * element:4 * element + 5, 4 * element:4 * element + 5] += stencil
        node_mass[4 * element:4 * element + 5] += weights
    return (assembled / node_mass[:, None])[:node_count, :node_count]

def radial_positions(node_count):
    gll_nodes, weights, derivative = gll_basis()
    positions = np.arange(node_count)
    return R_INNER + positions // 4 + 0.5 * (1.0 + gll_nodes[positions % 4])

def depth_derivative(fields):
    gll_nodes, weights, derivative = gll_basis()
    stencil = jnp.asarray(weights[:, None] * derivative * 2.0, fields.dtype)
    comps, depth_count, azim_count, radial_count = fields.shape
    elements = depth_count // 4
    extended = jnp.concatenate([fields, jnp.zeros_like(fields[:, :1])], axis=1)
    blocks = jnp.concatenate([fields.reshape(comps, elements, 4, azim_count, radial_count), extended[:, 4::4][:, :, None]], axis=2)
    contrib = jnp.einsum('ij,cejtr->ceitr', stencil, blocks, precision=HIGHEST)
    shifted = jnp.concatenate([jnp.zeros_like(contrib[:, :1, 4]), contrib[:, :-1, 4]], axis=1)
    first_node = contrib[:, :, 0] + shifted
    assembled = jnp.concatenate([first_node[:, :, None], contrib[:, :, 1:4]], axis=2)
    node_mass = np.tile(np.array([weights[0] + weights[4], weights[1], weights[2], weights[3]]), (elements, 1))
    node_mass[0, 0] = weights[0]
    node_mass = jnp.asarray(node_mass, fields.dtype)
    return (assembled / node_mass[None, :, :, None, None]).reshape(comps, depth_count, azim_count, radial_count)

def radial_derivative(fields):
    radial_matrix = jnp.asarray(radial_operator(fields.shape[3]), fields.dtype)
    return jnp.einsum('ij,cztj->czti', radial_matrix, fields, precision=HIGHEST)

def azimuth_derivative(fields):
    azim_count = fields.shape[2]
    spectrum = jnp.fft.rfft(fields, axis=2)
    mode_index = np.arange(azim_count // 2 + 1)
    wave_modes = np.where(mode_index == azim_count // 2, 0.0, mode_index * 1.0)
    return jnp.fft.irfft(1j * jnp.asarray(wave_modes)[:, None] * spectrum, n=azim_count, axis=2)

def reference(velocity, stress, memory, layer_ids, materials, jkd, source_depth):
    combined = jnp.concatenate([materials, jkd], axis=1)[layer_ids]
    per_node = jnp.repeat(jnp.repeat(combined, 4, axis=0), 4, axis=1)
    coeffs = jnp.moveaxis(per_node, 2, 0)[:, :, None, :]
    lame_zero, shear_mod, modulus, coupling = (coeffs[0], coeffs[1], coeffs[2], coeffs[3])
    density, fluid_density, tortuosity, friction = (coeffs[4], coeffs[5], coeffs[6], coeffs[7])
    relax_omega = coeffs[8]
    pole_weights = coeffs[9:13][:, None]
    pole_rates = coeffs[13:17][:, None]
    fluid_inertia = fluid_density * tortuosity
    determinant = density * fluid_inertia - fluid_density * fluid_density
    lame_fluid = lame_zero + coupling * coupling * modulus
    inverse_r = jnp.asarray(1.0 / radial_positions(NR), velocity.dtype)
    depth_total, azim_count = (velocity.shape[1], velocity.shape[2])
    plane_index = jnp.arange(depth_total, dtype=jnp.int32)
    source_mask = ((plane_index == source_depth[0])[:, None, None] & (jnp.arange(NR) < 4 * RB)[None, None, :]).astype(velocity.dtype)
    memory_state = memory.reshape(4, 3, depth_total, azim_count, NR)
    solid_vel, fluid_vel = (velocity[:3], velocity[3:])
    fields = stress
    for time_step in range(STEPS):
        radial_d = radial_derivative(jnp.stack([fields[0], fields[3], fields[4], fields[6]]))
        azim_d = azimuth_derivative(jnp.stack([fields[3], fields[1], fields[5], fields[6]])) * inverse_r
        depth_d = depth_derivative(jnp.stack([fields[4], fields[5], fields[2], fields[6]]))
        stress_div = jnp.stack([radial_d[0] + azim_d[0] + depth_d[0] + (fields[0] - fields[1]) * inverse_r, radial_d[1] + azim_d[1] + depth_d[1] + 2.0 * fields[3] * inverse_r, radial_d[2] + azim_d[2] + depth_d[2] + fields[4] * inverse_r])
        resist = jnp.stack([radial_d[3], azim_d[3], depth_d[3]]) + friction * lax.optimization_barrier(jnp.sum(pole_weights * memory_state, axis=0))
        solid_vel = solid_vel + DT * (fluid_inertia * stress_div + fluid_density * resist) / determinant
        fluid_step = -DT * (fluid_density * stress_div + density * resist) / determinant
        fluid_vel = fluid_vel + fluid_step
        memory_state = (memory_state + fluid_step + DT * relax_omega * fluid_vel) / (1.0 + DT * (pole_rates + relax_omega))
        radial_d = radial_derivative(jnp.stack([solid_vel[0], solid_vel[1], solid_vel[2], fluid_vel[0]]))
        azim_d = azimuth_derivative(jnp.stack([solid_vel[0], solid_vel[1], solid_vel[2], fluid_vel[1]])) * inverse_r
        depth_d = depth_derivative(jnp.stack([solid_vel[0], solid_vel[1], solid_vel[2], fluid_vel[2]]))
        strain_rr = radial_d[0]
        strain_tt = solid_vel[0] * inverse_r + azim_d[1]
        strain_zz = depth_d[2]
        shear_rt = azim_d[0] + radial_d[1] - solid_vel[1] * inverse_r
        shear_rz = depth_d[0] + radial_d[2]
        shear_tz = depth_d[1] + azim_d[2]
        div_solid = strain_rr + strain_tt + strain_zz
        div_fluid = radial_d[3] + fluid_vel[0] * inverse_r + azim_d[3] + depth_d[3]
        bulk_term = lame_fluid * div_solid + coupling * modulus * div_fluid
        source_term = DT * SOURCE_GAIN * math.cos(0.9 * time_step) * source_mask
        fields = jnp.stack([fields[0] + DT * (bulk_term + 2.0 * shear_mod * strain_rr), fields[1] + DT * (bulk_term + 2.0 * shear_mod * strain_tt), fields[2] + DT * (bulk_term + 2.0 * shear_mod * strain_zz), fields[3] + DT * shear_mod * shear_rt, fields[4] + DT * shear_mod * shear_rz, fields[5] + DT * shear_mod * shear_tz, fields[6] - DT * modulus * (coupling * div_solid + div_fluid) + source_term])
    velocity_out = jnp.concatenate([solid_vel, fluid_vel], axis=0)
    memory_out = memory_state.reshape(12, depth_total, azim_count, NR)
    return (velocity_out, fields, memory_out)
```

```python
import functools
import math

import jax
import jax.numpy as jnp
import numpy as np
from jax import lax
from jax.experimental import pallas as pl
from jax.experimental.pallas import tpu as pltpu
from jax.sharding import PartitionSpec as P

STEPS = 2
RB = 4


DT = 0.02
SOURCE_GAIN = 40.0
R_INNER = 1.0
MESH = pl.DeviceIdType.MESH
F32 = jnp.float32
BF16 = jnp.bfloat16


def gll_basis():
    root_value = math.sqrt(3.0 / 7.0)
    gll_nodes = np.array([-1.0, -root_value, 0.0, root_value, 1.0])
    weights = np.array([0.1, 49.0 / 90.0, 32.0 / 45.0, 49.0 / 90.0, 0.1])
    offsets = gll_nodes[:, None] - gll_nodes[None, :] + np.eye(5)
    factors = np.prod(offsets, axis=1)
    derivative = factors[:, None] / factors[None, :] / offsets
    diagonal_part = np.sum(1.0 / offsets, axis=1) - 1.0
    derivative = derivative * (1.0 - np.eye(5)) + np.eye(5) * diagonal_part[:, None]
    return (gll_nodes, weights, derivative)


def radial_operator(node_count):
    gll_nodes, weights, derivative = gll_basis()
    full_count = node_count + 1
    stencil = weights[:, None] * derivative * 2.0
    assembled = np.zeros((full_count, full_count))
    node_mass = np.zeros(full_count)
    for element in range(node_count // 4):
        assembled[4 * element : 4 * element + 5, 4 * element : 4 * element + 5] += stencil
        node_mass[4 * element : 4 * element + 5] += weights
    return (assembled / node_mass[:, None])[:node_count, :node_count]


def radial_positions(node_count):
    gll_nodes, weights, derivative = gll_basis()
    positions = np.arange(node_count)
    return R_INNER + positions // 4 + 0.5 * (1.0 + gll_nodes[positions % 4])


def azimuth_operator(node_count):
    positions = np.arange(node_count)
    offsets = positions[:, None] - positions[None, :]
    wave_modes = np.arange(1, node_count // 2)
    phases = 2.0 * np.pi * offsets[:, :, None] * wave_modes[None, None, :] / node_count
    return -(2.0 / node_count) * np.sum(wave_modes * np.sin(phases), axis=2)


def split_high_low(matrix):
    matrix = np.asarray(matrix, np.float32)
    high = matrix.astype(jnp.bfloat16)
    low = (matrix - high.astype(np.float32)).astype(jnp.bfloat16)
    return high, low


A1, A2, A3, FA, OM, INV, LF, BM, MU, PM, NCOEF = 0, 1, 2, 3, 7, 8, 12, 13, 14, 15, 16


def weighted(terms):
    total = None
    for factor, value in terms:
        if abs(factor) < 1e-12:
            continue
        term = value * np.float32(factor)
        total = term if total is None else total + term
    return total


def step_kernel(
    depth_devices, az_devices,
    mats, jkd, source, ids, expand, radial_k, azim_k, inv_r,
    vel_in, str_in, mem_in,
    vel_out, str_out, mem_out,
    s_az, s_rest, v_az, v_rest, mem, far, halo_above, halo_below, up_stage, down_stage,
    partial, coef, rad_d, az_d,
    load_sem, store_sem, az_send, az_recv, up_send, up_recv, down_send, down_recv,
):
    me_d = lax.axis_index("depth")
    me_a = lax.axis_index("az")
    depth, azims, radii = mem.shape[1:]
    chunks = depth // 4
    has_up = me_d < depth_devices - 1
    has_down = me_d > 0
    _, weights, derivative = gll_basis()
    stencil = weights[:, None] * derivative * 2.0

    def from_in(src, dst, index):
        return pltpu.make_async_copy(src, dst, load_sem.at[index])

    inner = pl.ds(0, depth)
    stress_place = [(s_rest, 0), (s_az, 1), (s_rest, 1), (s_az, 0), (s_rest, 2), (s_az, 2), (s_az, 3)]
    vel_place = [(v_az, 0), (v_az, 1), (v_az, 2), (v_rest, 0), (v_az, 3), (v_rest, 1)]
    loads = [from_in(str_in.at[i], ref.at[k, inner], i) for i, (ref, k) in enumerate(stress_place)]
    loads += [from_in(vel_in.at[i], ref.at[k, inner], 7 + i) for i, (ref, k) in enumerate(vel_place)]
    loads.append(from_in(mem_in, mem, 13))
    for copy in loads:
        copy.start()

    barrier = pltpu.get_barrier_semaphore()
    for k in range(1, az_devices):
        pl.semaphore_signal(
            barrier, inc=1, device_id=(me_d, lax.rem(me_a + k, az_devices)), device_id_type=MESH
        )

    @pl.when(has_up)
    def _():
        pl.semaphore_signal(barrier, inc=1, device_id=(me_d + 1, me_a), device_id_type=MESH)

    @pl.when(has_down)
    def _():
        pl.semaphore_signal(barrier, inc=1, device_id=(me_d - 1, me_a), device_id_type=MESH)

    ids_node = jnp.dot(
        ids[...].astype(F32).astype(BF16), expand[...], preferred_element_type=F32
    )

    def pick(table, column):
        value = jnp.zeros_like(ids_node)
        for row in range(8):
            value = jnp.where(ids_node == float(row), table[row, column], value)
        return value

    lame_zero, shear, modulus, coupling, rho, rho_f, tort, fric = [pick(mats, c) for c in range(8)]
    omega = pick(jkd, 0)
    rho_w = rho_f * tort
    scale = DT / (rho * rho_w - rho_f * rho_f)
    coef[A1] = rho_w * scale
    coef[A2] = rho_f * scale
    coef[A3] = rho * scale
    for pole in range(4):
        coef[FA + pole] = fric * pick(jkd, 1 + pole)
        coef[INV + pole] = 1.0 / (1.0 + DT * (pick(jkd, 5 + pole) + omega))
    coef[OM] = DT * omega
    coef[LF] = DT * (lame_zero + coupling * coupling * modulus)
    coef[BM] = DT * coupling * modulus
    coef[MU] = DT * shear
    coef[PM] = DT * modulus

    greeted = (az_devices - 1) + has_up.astype(jnp.int32) + has_down.astype(jnp.int32)
    pl.semaphore_wait(barrier, greeted)

    def az_copies(half, source_ref, e):
        planes = pl.ds(pl.multiple_of(4 * e, 4), 4)
        return [
            pltpu.make_async_remote_copy(
                src_ref=source_ref.at[:, planes],
                dst_ref=far.at[half, k - 1, :, planes],
                send_sem=az_send.at[half, k - 1, e],
                recv_sem=az_recv.at[half, k - 1, e],
                device_id=(me_d, lax.rem(me_a + az_devices - k, az_devices)),
                device_id_type=MESH,
            )
            for k in range(1, az_devices)
        ]

    def up_copy(half):
        return pltpu.make_async_remote_copy(
            src_ref=up_stage.at[half], dst_ref=halo_below.at[half],
            send_sem=up_send.at[half], recv_sem=up_recv.at[half],
            device_id=(me_d + 1, me_a), device_id_type=MESH,
        )

    def down_copy(half):
        return pltpu.make_async_remote_copy(
            src_ref=down_stage.at[half], dst_ref=halo_above.at[half],
            send_sem=down_send.at[half], recv_sem=down_recv.at[half],
            device_id=(me_d - 1, me_a), device_id_type=MESH,
        )

    stress_dz = [(s_rest, 2), (s_az, 2), (s_rest, 1), (s_az, 3)]
    vel_dz = [(v_az, 0), (v_az, 1), (v_az, 2), (v_rest, 1)]

    def top_of(ref, k, base):
        return weighted([(stencil[4, l], ref[k, base + l]) for l in range(4)])

    def send_down(half, dz_fields):
        for f, (ref, k) in enumerate(dz_fields):
            down_stage[half, f] = ref[k, 0]

        @pl.when(has_down)
        def _():
            down_copy(half).start()

    def send_up(half, dz_fields):
        for f, (ref, k) in enumerate(dz_fields):
            up_stage[half, f] = top_of(ref, k, depth - 4)

        @pl.when(has_up)
        def _():
            up_copy(half).start()

    def receive_halos(half, dz_fields):
        for e in range(1, chunks):
            for f, (ref, k) in enumerate(dz_fields):
                partial[f, e] = top_of(ref, k, 4 * (e - 1))

        @pl.when(has_up)
        def _():
            down_copy(half).wait_recv()
            for f, (ref, k) in enumerate(dz_fields):
                ref[k, depth] = halo_above[half, f]

        @pl.when(jnp.logical_not(has_up))
        def _():
            for f, (ref, k) in enumerate(dz_fields):
                ref[k, depth] = jnp.zeros((azims, radii), F32)

        @pl.when(has_down)
        def _():
            up_copy(half).wait_recv()
            partial[:, 0] = halo_below[half]

        @pl.when(jnp.logical_not(has_down))
        def _():
            for f, (ref, k) in enumerate(dz_fields):
                partial[f, 0] = weighted(
                    [(stencil[0, l] * (2.0 if l == 0 else 1.0), ref[k, l]) for l in range(5)]
                )

    def finish_sends(half, source_ref):
        for e in range(chunks):
            for copy in az_copies(half, source_ref, e):
                copy.wait_send()

        @pl.when(has_up)
        def _():
            up_copy(half).wait_send()

        @pl.when(has_down)
        def _():
            down_copy(half).wait_send()

    def dz_at(ref, k, f, base, e, j):
        if j == 0:
            total = weighted([(stencil[0, l], ref[k, base + l]) for l in range(1, 5)])
            return (total + partial[f, e]) * np.float32(1.0 / (2.0 * weights[0]))
        return weighted([(2.0 * derivative[j, l], ref[k, base + l]) for l in range(5)])

    def high_low(value, axis):
        high = value.astype(BF16)
        low = (value - high.astype(F32)).astype(BF16)
        return jnp.concatenate([high, low, high], axis=axis)

    def radial_part(refs, base):
        planes = pl.ds(base, 4)
        rows = jnp.concatenate(
            [ref[k, planes].reshape(4 * azims, radii) for ref, k in refs], axis=0
        )
        result = jnp.dot(high_low(rows, 1), radial_k[...], preferred_element_type=F32)
        rad_d[...] = result.reshape(4, 4, azims, radii)

    def azimuth_part(half, ref, base):
        for j in range(4):
            blocks = [jnp.concatenate([ref[f, base + j] for f in range(4)], axis=1)]
            for k in range(az_devices - 1):
                blocks.append(
                    jnp.concatenate([far[half, k, f, base + j] for f in range(4)], axis=1)
                )
            column = jnp.concatenate(blocks, axis=0)
            az_d[j] = jnp.dot(azim_k[...], high_low(column, 0), preferred_element_type=F32)

    def az_at(j, f):
        return az_d[j, :, f * radii : (f + 1) * radii]

    def row_of(e):
        def row(index):
            return coef[index, pl.ds(e, 1), :]

        return row

    def velocity_chunk(half, e):
        base = pl.multiple_of(4 * e, 4)
        for copy in az_copies(half, s_az, e):
            copy.wait_recv()
        radial_part([(s_rest, 0), (s_az, 0), (s_rest, 2), (s_az, 3)], base)
        azimuth_part(half, s_az, base)
        row = row_of(e)
        q = inv_r[...]
        for j in range(4):
            z = base + j
            rt, tt = s_az[0, z], s_az[1, z]
            rr, rz = s_rest[0, z], s_rest[2, z]
            dz = [dz_at(ref, k, f, base, e, j) for f, (ref, k) in enumerate(stress_dz)]
            div = [
                rad_d[0, j] + q * (az_at(j, 0) + (rr - tt)) + dz[0],
                rad_d[1, j] + q * (az_at(j, 1) + 2.0 * rt) + dz[1],
                rad_d[2, j] + q * (az_at(j, 2) + rz) + dz[2],
            ]
            grad = [rad_d[3, j], q * az_at(j, 3), dz[3]]
            solid = [(v_az, 0), (v_az, 1), (v_az, 2)]
            fluid = [(v_rest, 0), (v_az, 3), (v_rest, 1)]
            for c in range(3):
                psi = [mem[3 * pole + c, z] for pole in range(4)]
                resist = grad[c]
                for pole in range(4):
                    resist = resist + row(FA + pole) * psi[pole]
                ref, k = solid[c]
                ref[k, z] = ref[k, z] + (row(A1) * div[c] + row(A2) * resist)
                change = -(row(A2) * div[c] + row(A3) * resist)
                ref, k = fluid[c]
                fresh = ref[k, z] + change
                ref[k, z] = fresh
                change = change + row(OM) * fresh
                for pole in range(4):
                    mem[3 * pole + c, z] = (psi[pole] + change) * row(INV + pole)

    def stress_chunk(half, step, e):
        base = pl.multiple_of(4 * e, 4)
        for copy in az_copies(half, v_az, e):
            copy.wait_recv()
        radial_part([(v_az, 0), (v_az, 1), (v_az, 2), (v_rest, 0)], base)
        azimuth_part(half, v_az, base)
        row = row_of(e)
        q = inv_r[...]
        gain = np.float32(DT * SOURCE_GAIN * math.cos(0.9 * step))
        lane = lax.broadcasted_iota(jnp.int32, (1, radii), 1)
        wanted = jnp.zeros((1, radii), jnp.int32) + source[0]
        for j in range(4):
            z = base + j
            vr, vt, wr = v_az[0, z], v_az[1, z], v_rest[0, z]
            dz = [dz_at(ref, k, f, base, e, j) for f, (ref, k) in enumerate(vel_dz)]
            e_rr = rad_d[0, j]
            e_tt = q * (vr + az_at(j, 1))
            e_zz = dz[2]
            g_rt = q * (az_at(j, 0) - vt) + rad_d[1, j]
            g_rz = dz[0] + rad_d[2, j]
            g_tz = dz[1] + q * az_at(j, 2)
            div_v = e_rr + e_tt + e_zz
            div_w = rad_d[3, j] + q * (wr + az_at(j, 3)) + dz[3]
            bulk = row(LF) * div_v + row(BM) * div_w
            twice = 2.0 * row(MU)
            s_rest[0, z] = s_rest[0, z] + (bulk + twice * e_rr)
            s_az[1, z] = s_az[1, z] + (bulk + twice * e_tt)
            s_rest[1, z] = s_rest[1, z] + (bulk + twice * e_zz)
            s_az[0, z] = s_az[0, z] + row(MU) * g_rt
            s_rest[2, z] = s_rest[2, z] + row(MU) * g_rz
            s_az[2, z] = s_az[2, z] + row(MU) * g_tz
            plane = me_d * depth + z
            shot = jnp.where((wanted == plane) & (lane < 4 * RB), gain, np.float32(0.0))
            s_az[3, z] = s_az[3, z] - (row(BM) * div_v + row(PM) * div_w) + shot

    def start_az(half, ref, e):
        for copy in az_copies(half, ref, e):
            copy.start()

    for index in (1, 3, 5, 6):
        loads[index].wait()
    for e in range(chunks):
        start_az(0, s_az, e)
    for index in (0, 2, 4):
        loads[index].wait()
    send_down(0, stress_dz)
    send_up(0, stress_dz)
    for index in range(7, 14):
        loads[index].wait()

    stores = []

    def to_out(src, dst):
        copy = pltpu.make_async_copy(src, dst, store_sem.at[len(stores)])
        copy.start()
        stores.append(copy)

    for step in range(STEPS):
        half = 2 * step
        receive_halos(half, stress_dz)

        def velocity_body(e, carry):
            velocity_chunk(half, e)
            start_az(half + 1, v_az, e)

            @pl.when(e == 0)
            def _():
                send_down(half + 1, vel_dz)

            return carry

        lax.fori_loop(0, chunks, velocity_body, 0)
        send_up(half + 1, vel_dz)
        finish_sends(half, s_az)
        if step == STEPS - 1:
            to_out(mem, mem_out)
            for i, (ref, k) in enumerate(vel_place):
                to_out(ref.at[k, inner], vel_out.at[i])
        receive_halos(half + 1, vel_dz)

        def stress_body(e, carry):
            stress_chunk(half + 1, step, e)
            if step < STEPS - 1:
                start_az(half + 2, s_az, e)

                @pl.when(e == 0)
                def _():
                    send_down(half + 2, stress_dz)

            return carry

        lax.fori_loop(0, chunks, stress_body, 0)
        if step < STEPS - 1:
            send_up(half + 2, stress_dz)
        finish_sends(half + 1, v_az)
    for i, (ref, k) in enumerate(stress_place):
        to_out(ref.at[k, inner], str_out.at[i])
    for copy in stores:
        copy.wait()


def on_device(depth_devices, az_devices, velocity, stress, memory, layer_ids, materials, jkd, source_depth):
    depth, azims, radii = velocity.shape[1:]
    chunks = depth // 4
    halves = 2 * STEPS
    others = max(az_devices - 1, 1)
    azim_total = azims * az_devices
    radial_high, radial_low = split_high_low(radial_operator(radii).T)
    radial_k = np.concatenate([radial_high, radial_high, radial_low], axis=0)
    azim_high, azim_low = split_high_low(azimuth_operator(azim_total)[:azims])
    azim_k = np.concatenate([azim_high, azim_high, azim_low], axis=1)
    expand = np.kron(np.eye(radii // 4), np.ones((1, 4))).astype(jnp.bfloat16)
    inverse_r = (1.0 / radial_positions(radii)).astype(np.float32)[None]
    plane = (azims, radii)
    vmem = pl.BlockSpec(memory_space=pltpu.VMEM)
    smem = pl.BlockSpec(memory_space=pltpu.SMEM)
    hbm = pl.BlockSpec(memory_space=pl.ANY)
    dma = pltpu.SemaphoreType.DMA
    return tuple(pl.pallas_call(
        functools.partial(step_kernel, depth_devices, az_devices),
        out_shape=tuple(jax.ShapeDtypeStruct(x.shape, x.dtype) for x in (velocity, stress, memory)),
        in_specs=[smem, smem, smem, vmem, vmem, vmem, vmem, vmem, hbm, hbm, hbm],
        out_specs=(hbm, hbm, hbm),
        scratch_shapes=[
            pltpu.VMEM((4, depth + 1) + plane, F32),
            pltpu.VMEM((3, depth + 1) + plane, F32),
            pltpu.VMEM((4, depth + 1) + plane, F32),
            pltpu.VMEM((2, depth + 1) + plane, F32),
            pltpu.VMEM((12, depth) + plane, F32),
            pltpu.VMEM((halves, others, 4, depth) + plane, F32),
            pltpu.VMEM((halves, 4) + plane, F32),
            pltpu.VMEM((halves, 4) + plane, F32),
            pltpu.VMEM((halves, 4) + plane, F32),
            pltpu.VMEM((halves, 4) + plane, F32),
            pltpu.VMEM((4, chunks) + plane, F32),
            pltpu.VMEM((NCOEF, chunks, radii), F32),
            pltpu.VMEM((4, 4) + plane, F32),
            pltpu.VMEM((4, azims, 4 * radii), F32),
            dma((14,)),
            dma((14,)),
            dma((halves, others, chunks)),
            dma((halves, others, chunks)),
            dma((halves,)),
            dma((halves,)),
            dma((halves,)),
            dma((halves,)),
        ],
        compiler_params=pltpu.CompilerParams(
            collective_id=0, has_side_effects=True, vmem_limit_bytes=40 * 1024 * 1024
        ),
        cost_estimate=pl.CostEstimate(flops=10**9, bytes_accessed=2 * 25 * velocity.size // 6 * 4, transcendentals=0),
        name="biot_steps",
    )(
        materials, jkd, source_depth, layer_ids, jnp.asarray(expand), jnp.asarray(radial_k),
        jnp.asarray(azim_k), jnp.asarray(inverse_r), velocity, stress, memory,
    ))


def solution(mesh):
    return jax.shard_map(
        functools.partial(on_device, mesh.shape["depth"], mesh.shape["az"]),
        mesh=mesh,
        in_specs=(
            P(None, "depth", "az", None),
            P(None, "depth", "az", None),
            P(None, "depth", "az", None),
            P("depth", None),
            P(),
            P(),
            P(),
        ),
        out_specs=(
            P(None, "depth", "az", None),
            P(None, "depth", "az", None),
            P(None, "depth", "az", None),
        ),
        check_vma=False,
    )
```

```python
import functools
import math

import jax
import jax.numpy as jnp
import numpy as np
from jax import lax
from jax.experimental import pallas as pl
from jax.experimental.pallas import tpu as pltpu
from jax.sharding import PartitionSpec as P

STEPS = 2
RB = 4


DT = 0.02
SOURCE_GAIN = 40.0
R_INNER = 1.0
MESH = pl.DeviceIdType.MESH
F32 = jnp.float32
BF16 = jnp.bfloat16


def gll_basis():
    root_value = math.sqrt(3.0 / 7.0)
    gll_nodes = np.array([-1.0, -root_value, 0.0, root_value, 1.0])
    weights = np.array([0.1, 49.0 / 90.0, 32.0 / 45.0, 49.0 / 90.0, 0.1])
    offsets = gll_nodes[:, None] - gll_nodes[None, :] + np.eye(5)
    factors = np.prod(offsets, axis=1)
    derivative = factors[:, None] / factors[None, :] / offsets
    diagonal_part = np.sum(1.0 / offsets, axis=1) - 1.0
    derivative = derivative * (1.0 - np.eye(5)) + np.eye(5) * diagonal_part[:, None]
    return (gll_nodes, weights, derivative)


def radial_operator(node_count):
    gll_nodes, weights, derivative = gll_basis()
    full_count = node_count + 1
    stencil = weights[:, None] * derivative * 2.0
    assembled = np.zeros((full_count, full_count))
    node_mass = np.zeros(full_count)
    for element in range(node_count // 4):
        assembled[4 * element : 4 * element + 5, 4 * element : 4 * element + 5] += stencil
        node_mass[4 * element : 4 * element + 5] += weights
    return (assembled / node_mass[:, None])[:node_count, :node_count]


def radial_positions(node_count):
    gll_nodes, weights, derivative = gll_basis()
    positions = np.arange(node_count)
    return R_INNER + positions // 4 + 0.5 * (1.0 + gll_nodes[positions % 4])


def azimuth_operator(node_count):
    positions = np.arange(node_count)
    offsets = positions[:, None] - positions[None, :]
    wave_modes = np.arange(1, node_count // 2)
    phases = 2.0 * np.pi * offsets[:, :, None] * wave_modes[None, None, :] / node_count
    return -(2.0 / node_count) * np.sum(wave_modes * np.sin(phases), axis=2)


def split_high_low(matrix):
    matrix = np.asarray(matrix, np.float32)
    high = matrix.astype(jnp.bfloat16)
    low = (matrix - high.astype(np.float32)).astype(jnp.bfloat16)
    return high, low


A1, A2, A3, FA, OM, INV, LF, BM, MU, PM, NCOEF = 0, 1, 2, 3, 7, 8, 12, 13, 14, 15, 16


def weighted(terms):
    total = None
    for factor, value in terms:
        if abs(factor) < 1e-12:
            continue
        term = value * np.float32(factor)
        total = term if total is None else total + term
    return total


def step_kernel(
    depth_devices, az_devices,
    source, mats_in, jkd_in, ids_in, expand_in, radial_in, azim_in, inv_r_in, vel_in, str_in, mem_in,
    vel_out, str_out, mem,
    mats, jkd, ids, expand, radial_k, azim_k, inv_r,
    s_az, s_rest, v_az, v_rest, far_s, far_v, far_new, far_dw, far_psi, far_dt, dw, psi_t,
    halo_above, halo_below, far_above, far_below, up_stage, down_stage,
    partial, far_partial, coef, rad_d, az_d,
    load_sem, store_sem, az_send, az_recv, up_send, up_recv, down_send, down_recv,
):
    me_d = lax.axis_index("depth")
    me_a = lax.axis_index("az")
    depth, azims, radii = mem.shape[1:]
    chunks = depth // 4
    others = range(az_devices - 1)
    has_up = me_d < depth_devices - 1
    has_down = me_d > 0
    _, weights, derivative = gll_basis()
    stencil = weights[:, None] * derivative * 2.0

    inner = pl.ds(0, depth)
    stress_place = [(s_rest, 0), (s_az, 1), (s_rest, 1), (s_az, 0), (s_rest, 2), (s_az, 2), (s_az, 3)]
    vel_place = [(v_az, 0), (v_az, 2), (v_az, 1), (v_rest, 0), (v_az, 3), (v_rest, 1)]
    pairs = [(str_in.at[i], ref.at[k, inner]) for i, (ref, k) in enumerate(stress_place)]
    pairs += [(vel_in.at[i], ref.at[k, inner]) for i, (ref, k) in enumerate(vel_place)]
    pairs += [(mem_in, mem), (mats_in, mats), (jkd_in, jkd), (ids_in, ids), (expand_in, expand)]
    pairs += [(radial_in, radial_k), (azim_in, azim_k), (inv_r_in, inv_r)]
    loads = [
        pltpu.make_async_copy(src, dst, load_sem.at[i]) for i, (src, dst) in enumerate(pairs)
    ]
    for index in (1, 3, 5, 6, 14, 15, 16, 17, 0, 2, 4, 18, 19, 20, 7, 8, 9, 10, 11, 12, 13):
        loads[index].start()

    def other_az(k, sign):
        return lax.rem(me_a + (az_devices + sign * k), az_devices)

    barrier = pltpu.get_barrier_semaphore()

    def greet(where_d, where_a):
        pl.semaphore_signal(barrier, inc=1, device_id=(where_d, where_a), device_id_type=MESH)

    for k in range(1, az_devices):
        greet(me_d, other_az(k, 1))

    @pl.when(has_up)
    def _():
        for k in range(az_devices):
            greet(me_d + 1, other_az(k, 1))

    @pl.when(has_down)
    def _():
        for k in range(az_devices):
            greet(me_d - 1, other_az(k, 1))

    neighbours = has_up.astype(jnp.int32) + has_down.astype(jnp.int32)
    pl.semaphore_wait(barrier, (az_devices - 1) + az_devices * neighbours)

    exchanges = [
        (s_az, far_s, 4), (v_az, far_v, 4), (psi_t, far_psi, 1), (dw, far_dw, 1), (v_az, far_new, 2),
    ]

    def az_copies(which, e):
        source_ref, target_ref, count = exchanges[which]
        planes = pl.ds(pl.multiple_of(4 * e, 4), 4)
        return [
            pltpu.make_async_remote_copy(
                src_ref=source_ref.at[pl.ds(0, count), planes],
                dst_ref=target_ref.at[k, pl.ds(0, count), planes],
                send_sem=az_send.at[which, k, e],
                recv_sem=az_recv.at[which, k, e],
                device_id=(me_d, other_az(k + 1, -1)),
                device_id_type=MESH,
            )
            for k in others
        ]

    def start_az(which, e):
        for copy in az_copies(which, e):
            copy.start()

    def receive_az(which, e):
        for copy in az_copies(which, e):
            copy.wait_recv()

    far_fields = {1: (1, 2), 2: (1, 1)}

    def halo_copies(half, stage, near, far, send_sem, recv_sem, where_d):
        copies = [
            pltpu.make_async_remote_copy(
                src_ref=stage.at[half], dst_ref=near.at[half],
                send_sem=send_sem.at[half, 0], recv_sem=recv_sem.at[half, 0],
                device_id=(where_d, me_a), device_id_type=MESH,
            )
        ]
        if half in far_fields:
            first, count = far_fields[half]
            for k in others:
                copies.append(
                    pltpu.make_async_remote_copy(
                        src_ref=stage.at[half, pl.ds(first, count)],
                        dst_ref=far.at[half - 1, k, pl.ds(0, count)],
                        send_sem=send_sem.at[half, k + 1], recv_sem=recv_sem.at[half, k + 1],
                        device_id=(where_d, other_az(k + 1, -1)), device_id_type=MESH,
                    )
                )
        return copies

    def up_copies(half):
        return halo_copies(half, up_stage, halo_below, far_below, up_send, up_recv, me_d + 1)

    def down_copies(half):
        return halo_copies(half, down_stage, halo_above, far_above, down_send, down_recv, me_d - 1)

    stress_dz = [(s_rest, 2), (s_az, 2), (s_rest, 1), (s_az, 3)]
    vel_dz = [(v_az, 0), (v_az, 1), (v_az, 2), (v_rest, 1)]

    def top_of(read, base):
        return weighted([(stencil[4, l], read(base + l)) for l in range(4)])

    def bottom_of(read):
        return weighted([(stencil[0, l] * (2.0 if l == 0 else 1.0), read(l)) for l in range(5)])

    def reader(ref, k):
        return lambda z: ref[k, z]

    def far_reader(ref, k, f):
        return lambda z: ref[k, f, z]

    def send_down(half, dz_fields):
        for f, (ref, k) in enumerate(dz_fields):
            down_stage[half, f] = ref[k, 0]

        @pl.when(has_down)
        def _():
            for copy in down_copies(half):
                copy.start()

    def send_up(half, dz_fields):
        for f, (ref, k) in enumerate(dz_fields):
            up_stage[half, f] = top_of(reader(ref, k), depth - 4)

        @pl.when(has_up)
        def _():
            for copy in up_copies(half):
                copy.start()

    def receive_halos(half, dz_fields):
        for e in range(1, chunks):
            for f, (ref, k) in enumerate(dz_fields):
                partial[f, e] = top_of(reader(ref, k), 4 * (e - 1))

        @pl.when(has_up)
        def _():
            down_copies(half)[0].wait_recv()
            for f, (ref, k) in enumerate(dz_fields):
                ref[k, depth] = halo_above[half, f]

        @pl.when(jnp.logical_not(has_up))
        def _():
            for f, (ref, k) in enumerate(dz_fields):
                ref[k, depth] = jnp.zeros((azims, radii), F32)

        @pl.when(has_down)
        def _():
            up_copies(half)[0].wait_recv()
            partial[:, 0] = halo_below[half]

        @pl.when(jnp.logical_not(has_down))
        def _():
            for f, (ref, k) in enumerate(dz_fields):
                partial[f, 0] = bottom_of(reader(ref, k))

    def receive_far_halos(half, ref):
        first, count = far_fields[half]
        fields = [(k, i, FAR_DZ[half][i]) for k in others for i in range(count)]
        for e in range(1, chunks):
            for k, i, f in fields:
                far_partial[k, i, e] = top_of(far_reader(ref, k, f), 4 * (e - 1))

        @pl.when(has_up)
        def _():
            for copy in down_copies(half)[1:]:
                copy.wait_recv()
            for k, i, f in fields:
                ref[k, f, depth] = far_above[half - 1, k, i]

        @pl.when(jnp.logical_not(has_up))
        def _():
            for k, i, f in fields:
                ref[k, f, depth] = jnp.zeros((azims, radii), F32)

        @pl.when(has_down)
        def _():
            for copy in up_copies(half)[1:]:
                copy.wait_recv()
            for k, i, f in fields:
                far_partial[k, i, 0] = far_below[half - 1, k, i]

        @pl.when(jnp.logical_not(has_down))
        def _():
            for k, i, f in fields:
                far_partial[k, i, 0] = bottom_of(far_reader(ref, k, f))

    def finish_az(which):
        for e in range(chunks):
            for copy in az_copies(which, e):
                copy.wait_send()

    def finish_halos(half):
        @pl.when(has_up)
        def _():
            for copy in up_copies(half):
                copy.wait_send()

        @pl.when(has_down)
        def _():
            for copy in down_copies(half):
                copy.wait_send()

    def dz_at(read, below, base, j):
        if j == 0:
            total = weighted([(stencil[0, l], read(base + l)) for l in range(1, 5)])
            return (total + below) * np.float32(1.0 / (2.0 * weights[0]))
        return weighted([(2.0 * derivative[j, l], read(base + l)) for l in range(5)])

    def high_low(value, axis):
        high = value.astype(BF16)
        low = (value - high.astype(F32)).astype(BF16)
        return jnp.concatenate([high, low, high], axis=axis)

    def radial_part(blocks):
        rows = jnp.concatenate([block.reshape(4 * azims, radii) for block in blocks], axis=0)
        result = jnp.dot(high_low(rows, 1), radial_k[...], preferred_element_type=F32)
        rad_d[0 : len(blocks)] = result.reshape(len(blocks), 4, azims, radii)

    def azimuth_part(near, far, base, kept):
        rows = azims * az_devices if kept else azims
        for j in range(4):
            blocks = [jnp.concatenate([ref[f, base + j] for ref, f in near], axis=1)]
            for k in others:
                blocks.append(jnp.concatenate([ref[k, f, base + j] for ref, f in far], axis=1))
            column = jnp.concatenate(blocks, axis=0)
            result = jnp.dot(
                azim_k[0:rows, :], high_low(column, 0), preferred_element_type=F32
            )
            az_d[j] = result[0:azims]
            for i, f in enumerate(kept):
                for k in others:
                    far_dt[k, i, base + j] = result[
                        (k + 1) * azims : (k + 2) * azims, f * radii : (f + 1) * radii
                    ]

    def az_at(j, f):
        return az_d[j, :, f * radii : (f + 1) * radii]

    def row_of(e):
        def row(index):
            return coef[index, pl.ds(e, 1), :]

        return row

    def shot_at(step, z):
        gain = np.float32(DT * SOURCE_GAIN * math.cos(0.9 * step))
        lane = lax.broadcasted_iota(jnp.int32, (1, radii), 1)
        wanted = jnp.zeros((1, radii), jnp.int32) + source[0]
        return jnp.where((wanted == me_d * depth + z) & (lane < 4 * RB), gain, np.float32(0.0))

    def velocity_chunk(step, e):
        base = pl.multiple_of(4 * e, 4)
        planes = pl.ds(base, 4)
        row = row_of(e)
        if step == 0:
            receive_az(0, e)
        else:
            receive_az(3, e)
            for k in others:
                for j in range(4):
                    z = base + j
                    far_s[k, 1, z] = far_s[k, 1, z] + row(BM) * far_dw[k, 0, z]
                    far_s[k, 3, z] = far_s[k, 3, z] - row(PM) * far_dw[k, 0, z]
        radial_part([s_rest[0, planes], s_az[0, planes], s_rest[2, planes], s_az[3, planes]])
        azimuth_part(
            [(s_az, f) for f in range(4)], [(far_s, f) for f in range(4)], base,
            (1, 3) if step == 1 else (),
        )
        q = inv_r[...]
        for j in range(4):
            z = base + j
            rt, tt = s_az[0, z], s_az[1, z]
            rr, rz = s_rest[0, z], s_rest[2, z]
            dz = [
                dz_at(reader(ref, k), partial[f, e], base, j)
                for f, (ref, k) in enumerate(stress_dz)
            ]
            div = [
                rad_d[0, j] + q * (az_at(j, 0) + (rr - tt)) + dz[0],
                rad_d[1, j] + q * (az_at(j, 1) + 2.0 * rt) + dz[1],
                rad_d[2, j] + q * (az_at(j, 2) + rz) + dz[2],
            ]
            grad = [rad_d[3, j], q * az_at(j, 3), dz[3]]
            solid = [(v_az, 0), (v_az, 2), (v_az, 1)]
            fluid = [(v_rest, 0), (v_az, 3), (v_rest, 1)]
            for c in range(3):
                psi = [mem[3 * pole + c, z] for pole in range(4)]
                resist = grad[c]
                for pole in range(4):
                    resist = resist + row(FA + pole) * psi[pole]
                ref, k = solid[c]
                ref[k, z] = ref[k, z] + (row(A1) * div[c] + row(A2) * resist)
                change = -(row(A2) * div[c] + row(A3) * resist)
                ref, k = fluid[c]
                fresh = ref[k, z] + change
                ref[k, z] = fresh
                change = change + row(OM) * fresh
                psi = [(psi[pole] + change) * row(INV + pole) for pole in range(4)]
                for pole in range(4):
                    mem[3 * pole + c, z] = psi[pole]
                if c == 1 and step == 0:
                    total = row(FA) * psi[0]
                    for pole in range(1, 4):
                        total = total + row(FA + pole) * psi[pole]
                    psi_t[0, z] = total

    def stress_chunk(step, e):
        base = pl.multiple_of(4 * e, 4)
        planes = pl.ds(base, 4)
        radial_part([v_az[0, planes], v_az[2, planes], v_az[1, planes], v_rest[0, planes]])
        if step == 0:
            receive_az(1, e)
            far = [(far_v, f) for f in range(4)]
        else:
            receive_az(4, e)
            far = [(far_new, 0), (far_new, 1), (far_v, 2), (far_v, 3)]
        azimuth_part([(v_az, f) for f in range(4)], far, base, (0, 1, 2) if step == 0 else ())
        row = row_of(e)
        q = inv_r[...]
        for j in range(4):
            z = base + j
            vr, vt, wr = v_az[0, z], v_az[2, z], v_rest[0, z]
            dz = [
                dz_at(reader(ref, k), partial[f, e], base, j)
                for f, (ref, k) in enumerate(vel_dz)
            ]
            e_rr = rad_d[0, j]
            e_tt = q * (vr + az_at(j, 2))
            e_zz = dz[1]
            g_rt = q * (az_at(j, 0) - vt) + rad_d[1, j]
            g_rz = dz[0] + rad_d[2, j]
            g_tz = dz[2] + q * az_at(j, 1)
            div_v = e_rr + e_tt + e_zz
            div_w = rad_d[3, j] + q * (wr + az_at(j, 3)) + dz[3]
            if step == 0:
                dw[0, z] = div_w
            bulk = row(LF) * div_v + row(BM) * div_w
            twice = 2.0 * row(MU)
            s_rest[0, z] = s_rest[0, z] + (bulk + twice * e_rr)
            s_az[1, z] = s_az[1, z] + (bulk + twice * e_tt)
            s_rest[1, z] = s_rest[1, z] + (bulk + twice * e_zz)
            s_az[0, z] = s_az[0, z] + row(MU) * g_rt
            s_rest[2, z] = s_rest[2, z] + row(MU) * g_rz
            s_az[2, z] = s_az[2, z] + row(MU) * g_tz
            s_az[3, z] = s_az[3, z] - (row(BM) * div_v + row(PM) * div_w) + shot_at(step, z)

    def far_stress_chunk(e):
        base = pl.multiple_of(4 * e, 4)
        planes = pl.ds(base, 4)
        row = row_of(e)
        q = inv_r[...]
        for k in others:
            radial_part([far_v[k, 0, planes], far_v[k, 2, planes]])
            for j in range(4):
                z = base + j
                vr, vt = far_v[k, 0, z], far_v[k, 2, z]
                dz_vz = dz_at(far_reader(far_v, k, 1), far_partial[k, 0, e], base, j)
                dz_vt = dz_at(far_reader(far_v, k, 2), far_partial[k, 1, e], base, j)
                e_tt = q * (vr + far_dt[k, 2, z])
                div_v = rad_d[0, j] + e_tt + dz_vz
                g_rt = q * (far_dt[k, 0, z] - vt) + rad_d[1, j]
                g_tz = dz_vt + q * far_dt[k, 1, z]
                far_s[k, 0, z] = far_s[k, 0, z] + row(MU) * g_rt
                far_s[k, 1, z] = far_s[k, 1, z] + (row(LF) * div_v + 2.0 * row(MU) * e_tt)
                far_s[k, 2, z] = far_s[k, 2, z] + row(MU) * g_tz
                far_s[k, 3, z] = far_s[k, 3, z] - row(BM) * div_v + shot_at(0, z)

    def far_velocity_chunk(e):
        base = pl.multiple_of(4 * e, 4)
        planes = pl.ds(base, 4)
        row = row_of(e)
        q = inv_r[...]
        receive_az(2, e)
        for k in others:
            radial_part([far_s[k, 0, planes]])
            for j in range(4):
                z = base + j
                dz_tz = dz_at(far_reader(far_s, k, 2), far_partial[k, 0, e], base, j)
                div = rad_d[0, j] + q * (far_dt[k, 0, z] + 2.0 * far_s[k, 0, z]) + dz_tz
                resist = q * far_dt[k, 1, z] + far_psi[k, 0, z]
                far_v[k, 2, z] = far_v[k, 2, z] + (row(A1) * div + row(A2) * resist)
                far_v[k, 3, z] = far_v[k, 3, z] - (row(A2) * div + row(A3) * resist)

    def each_chunk(body):
        def wrapped(e, carry):
            body(e)
            return carry

        lax.fori_loop(0, chunks, wrapped, 0)

    for index in (1, 3, 5, 6):
        loads[index].wait()
    for e in range(chunks):
        start_az(0, e)
    for index in (0, 2, 4):
        loads[index].wait()
    send_down(0, stress_dz)
    send_up(0, stress_dz)
    for index in range(14, 21):
        loads[index].wait()

    ids_node = jnp.dot(
        ids[...].astype(F32).astype(BF16), expand[...], preferred_element_type=F32
    )

    def pick(table, column):
        value = jnp.zeros_like(ids_node)
        for r in range(8):
            value = jnp.where(ids_node == float(r), table[r : r + 1, column : column + 1], value)
        return value

    lame_zero, shear, modulus, coupling, rho, rho_f, tort, fric = [pick(mats, c) for c in range(8)]
    omega = pick(jkd, 0)
    rho_w = rho_f * tort
    scale = DT / (rho * rho_w - rho_f * rho_f)
    coef[A1] = rho_w * scale
    coef[A2] = rho_f * scale
    coef[A3] = rho * scale
    for pole in range(4):
        coef[FA + pole] = fric * pick(jkd, 1 + pole)
        coef[INV + pole] = 1.0 / (1.0 + DT * (pick(jkd, 5 + pole) + omega))
    coef[OM] = DT * omega
    coef[LF] = DT * (lame_zero + coupling * coupling * modulus)
    coef[BM] = DT * coupling * modulus
    coef[MU] = DT * shear
    coef[PM] = DT * modulus

    for index in range(7, 14):
        loads[index].wait()

    stores = []

    def to_out(src, dst):
        copy = pltpu.make_async_copy(src, dst, store_sem.at[len(stores)])
        copy.start()
        stores.append(copy)

    receive_halos(0, stress_dz)

    def first_velocity(e):
        velocity_chunk(0, e)
        start_az(1, e)

        @pl.when(e == 0)
        def _():
            send_down(1, vel_dz)

    each_chunk(first_velocity)
    send_up(1, vel_dz)
    for e in range(chunks):
        start_az(2, e)
    finish_az(0)
    finish_halos(0)

    receive_halos(1, vel_dz)

    def first_stress(e):
        stress_chunk(0, e)
        start_az(3, e)

        @pl.when(e == 0)
        def _():
            send_down(2, stress_dz)

    each_chunk(first_stress)
    send_up(2, stress_dz)
    receive_far_halos(1, far_v)
    each_chunk(far_stress_chunk)
    finish_az(1)
    finish_halos(1)

    receive_halos(2, stress_dz)

    def second_velocity(e):
        velocity_chunk(1, e)
        start_az(4, e)

        @pl.when(e == 0)
        def _():
            send_down(3, vel_dz)

    each_chunk(second_velocity)
    send_up(3, vel_dz)
    for i, (ref, k) in enumerate(vel_place):
        to_out(ref.at[k, inner], vel_out.at[i])
    receive_far_halos(2, far_s)
    each_chunk(far_velocity_chunk)
    finish_az(2)
    finish_az(3)
    finish_halos(2)

    receive_halos(3, vel_dz)
    each_chunk(lambda e: stress_chunk(1, e))
    for i, (ref, k) in enumerate(stress_place):
        to_out(ref.at[k, inner], str_out.at[i])
    finish_az(4)
    finish_halos(3)
    for copy in stores:
        copy.wait()


FAR_DZ = {1: (1, 2), 2: (2,)}


def on_device(depth_devices, az_devices, velocity, stress, memory, layer_ids, materials, jkd, source_depth):
    depth, azims, radii = velocity.shape[1:]
    chunks = depth // 4
    halves = 2 * STEPS
    others = max(az_devices - 1, 1)
    azim_total = azims * az_devices
    radial_high, radial_low = split_high_low(radial_operator(radii).T)
    radial_k = np.concatenate([radial_high, radial_high, radial_low], axis=0)
    azim_high, azim_low = split_high_low(azimuth_operator(azim_total))
    azim_k = np.concatenate([azim_high, azim_high, azim_low], axis=1)
    expand = np.kron(np.eye(radii // 4), np.ones((1, 4))).astype(jnp.bfloat16)
    inverse_r = (1.0 / radial_positions(radii)).astype(np.float32)[None]
    plane = (azims, radii)
    smem = pl.BlockSpec(memory_space=pltpu.SMEM)
    hbm = pl.BlockSpec(memory_space=pltpu.HBM)
    anywhere = pl.BlockSpec(memory_space=pl.ANY)
    vmem = pl.BlockSpec(memory_space=pltpu.VMEM)
    dma = pltpu.SemaphoreType.DMA
    constants = [expand, radial_k, azim_k, inverse_r]
    small = [materials, jkd, layer_ids] + [jnp.asarray(value) for value in constants]

    def held(*shape):
        return pltpu.VMEM(shape + plane, F32)

    return tuple(pl.pallas_call(
        functools.partial(step_kernel, depth_devices, az_devices),
        out_shape=tuple(jax.ShapeDtypeStruct(x.shape, x.dtype) for x in (velocity, stress, memory)),
        in_specs=[smem] + [hbm] * 10,
        out_specs=(anywhere, anywhere, vmem),
        scratch_shapes=[pltpu.VMEM(value.shape, value.dtype) for value in small] + [
            held(4, depth + 1),
            held(3, depth + 1),
            held(4, depth + 1),
            held(2, depth + 1),
            held(others, 4, depth + 1),
            held(others, 4, depth + 1),
            held(others, 2, depth),
            held(others, 1, depth),
            held(others, 1, depth),
            held(others, 3, depth),
            held(1, depth),
            held(1, depth),
            held(halves, 4),
            held(halves, 4),
            held(2, others, 2),
            held(2, others, 2),
            held(halves, 4),
            held(halves, 4),
            held(4, chunks),
            held(others, 2, chunks),
            pltpu.VMEM((NCOEF, chunks, radii), F32),
            held(4, 4),
            pltpu.VMEM((4, azims, 4 * radii), F32),
            dma((21,)),
            dma((13,)),
            dma((5, others, chunks)),
            dma((5, others, chunks)),
            dma((halves, others + 1)),
            dma((halves, others + 1)),
            dma((halves, others + 1)),
            dma((halves, others + 1)),
        ],
        compiler_params=pltpu.CompilerParams(
            collective_id=0, has_side_effects=True, vmem_limit_bytes=40 * 1024 * 1024
        ),
        cost_estimate=pl.CostEstimate(
            flops=10**9, bytes_accessed=2 * 25 * velocity.size // 6 * 4, transcendentals=0
        ),
        name="biot_steps",
    )(source_depth, *small, velocity, stress, memory))


def solution(mesh):
    return jax.shard_map(
        functools.partial(on_device, mesh.shape["depth"], mesh.shape["az"]),
        mesh=mesh,
        in_specs=(
            P(None, "depth", "az", None),
            P(None, "depth", "az", None),
            P(None, "depth", "az", None),
            P("depth", None),
            P(),
            P(),
            P(),
        ),
        out_specs=(
            P(None, "depth", "az", None),
            P(None, "depth", "az", None),
            P(None, "depth", "az", None),
        ),
        check_vma=False,
    )
```

```python
import functools
import math

import jax
import jax.numpy as jnp
import numpy as np
from jax import lax
from jax.experimental import pallas as pl
from jax.experimental.pallas import tpu as pltpu
from jax.sharding import PartitionSpec as P

STEPS = 2
RB = 4


DT = 0.02
SOURCE_GAIN = 40.0
R_INNER = 1.0
MESH = pl.DeviceIdType.MESH
F32 = jnp.float32
BF16 = jnp.bfloat16


def gll_basis():
    root_value = math.sqrt(3.0 / 7.0)
    gll_nodes = np.array([-1.0, -root_value, 0.0, root_value, 1.0])
    weights = np.array([0.1, 49.0 / 90.0, 32.0 / 45.0, 49.0 / 90.0, 0.1])
    offsets = gll_nodes[:, None] - gll_nodes[None, :] + np.eye(5)
    factors = np.prod(offsets, axis=1)
    derivative = factors[:, None] / factors[None, :] / offsets
    diagonal_part = np.sum(1.0 / offsets, axis=1) - 1.0
    derivative = derivative * (1.0 - np.eye(5)) + np.eye(5) * diagonal_part[:, None]
    return (gll_nodes, weights, derivative)


def radial_operator(node_count):
    gll_nodes, weights, derivative = gll_basis()
    full_count = node_count + 1
    stencil = weights[:, None] * derivative * 2.0
    assembled = np.zeros((full_count, full_count))
    node_mass = np.zeros(full_count)
    for element in range(node_count // 4):
        assembled[4 * element : 4 * element + 5, 4 * element : 4 * element + 5] += stencil
        node_mass[4 * element : 4 * element + 5] += weights
    return (assembled / node_mass[:, None])[:node_count, :node_count]


def azimuth_operator(node_count):
    positions = np.arange(node_count)
    offsets = positions[:, None] - positions[None, :]
    wave_modes = np.arange(1, node_count // 2)
    phases = 2.0 * np.pi * offsets[:, :, None] * wave_modes[None, None, :] / node_count
    return -(2.0 / node_count) * np.sum(wave_modes * np.sin(phases), axis=2)


def split_high_low(matrix):
    matrix = np.asarray(matrix, np.float32)
    high = matrix.astype(jnp.bfloat16)
    low = (matrix - high.astype(np.float32)).astype(jnp.bfloat16)
    return high, low


A1, A2, A3, FA, OM, INV, LF, BM, MU, PM, NCOEF = 0, 1, 2, 3, 7, 8, 12, 13, 14, 15, 16


def weighted(terms):
    total = None
    for factor, value in terms:
        if abs(factor) < 1e-12:
            continue
        term = value * np.float32(factor)
        total = term if total is None else total + term
    return total


def step_kernel(
    depth_devices, az_devices,
    source, mats_in, jkd_in, ids_in, radial_in, azim_in, vel_in, str_in, mem_in,
    vel_out, str_out, mem_out,
    mats, jkd, ids, radial_k, azim_k,
    mem, inv_r, s_az, s_rest, v_az, v_rest, far_s, far_v, far_new, far_dw, far_psi, far_dt, dw, psi_t,
    halo_above, halo_below, far_above, far_below, up_stage, down_stage,
    partial, far_partial, coef, rad_d, az_d,
    load_sem, store_sem, chunk_sem, az_send, az_recv, up_send, up_recv, down_send, down_recv,
):
    me_d = lax.axis_index("depth")
    me_a = lax.axis_index("az")
    depth, azims, radii = mem.shape[1:]
    chunks = depth // 4
    others = range(az_devices - 1)
    has_up = me_d < depth_devices - 1
    has_down = me_d > 0
    gll_nodes, weights, derivative = gll_basis()
    stencil = weights[:, None] * derivative * 2.0

    inner = pl.ds(0, depth)
    stress_place = [(s_rest, 0), (s_az, 1), (s_rest, 1), (s_az, 0), (s_rest, 2), (s_az, 2), (s_az, 3)]
    vel_place = [(v_az, 0), (v_az, 2), (v_az, 1), (v_rest, 0), (v_az, 3), (v_rest, 1)]
    pairs = [(str_in.at[i], ref.at[k, inner]) for i, (ref, k) in enumerate(stress_place)]
    pairs += [(vel_in.at[i], ref.at[k, inner]) for i, (ref, k) in enumerate(vel_place)]
    pairs += [(mem_in, mem), (mats_in, mats), (jkd_in, jkd), (ids_in, ids)]
    pairs += [(radial_in, radial_k), (azim_in, azim_k)]
    loads = [
        pltpu.make_async_copy(src, dst, load_sem.at[i]) for i, (src, dst) in enumerate(pairs)
    ]
    for index in (1, 3, 5, 6, 14, 15, 16, 0, 2, 4, 17, 18, 7, 8, 9, 10, 11, 12, 13):
        loads[index].start()

    def other_az(k, sign):
        return lax.rem(me_a + (az_devices + sign * k), az_devices)

    barrier = pltpu.get_barrier_semaphore()

    def greet(where_d, where_a):
        pl.semaphore_signal(barrier, inc=1, device_id=(where_d, where_a), device_id_type=MESH)

    for k in range(1, az_devices):
        greet(me_d, other_az(k, 1))

    @pl.when(has_up)
    def _():
        for k in range(az_devices):
            greet(me_d + 1, other_az(k, 1))

    @pl.when(has_down)
    def _():
        for k in range(az_devices):
            greet(me_d - 1, other_az(k, 1))

    neighbours = has_up.astype(jnp.int32) + has_down.astype(jnp.int32)
    pl.semaphore_wait(barrier, (az_devices - 1) + az_devices * neighbours)

    exchanges = [
        (s_az, far_s, 4), (v_az, far_v, 4), (psi_t, far_psi, 1), (dw, far_dw, 1), (v_az, far_new, 2),
    ]

    def az_copies(which, e):
        source_ref, target_ref, count = exchanges[which]
        planes = pl.ds(pl.multiple_of(4 * e, 4), 4)
        return [
            pltpu.make_async_remote_copy(
                src_ref=source_ref.at[pl.ds(0, count), planes],
                dst_ref=target_ref.at[k, pl.ds(0, count), planes],
                send_sem=az_send.at[which, k, e],
                recv_sem=az_recv.at[which, k, e],
                device_id=(me_d, other_az(k + 1, -1)),
                device_id_type=MESH,
            )
            for k in others
        ]

    def start_az(which, e):
        for copy in az_copies(which, e):
            copy.start()

    def receive_az(which, e):
        for copy in az_copies(which, e):
            copy.wait_recv()

    far_fields = {1: (1, 2), 2: (1, 1)}

    def halo_copies(half, stage, near, far, send_sem, recv_sem, where_d):
        copies = [
            pltpu.make_async_remote_copy(
                src_ref=stage.at[half], dst_ref=near.at[half],
                send_sem=send_sem.at[half, 0], recv_sem=recv_sem.at[half, 0],
                device_id=(where_d, me_a), device_id_type=MESH,
            )
        ]
        if half in far_fields:
            first, count = far_fields[half]
            for k in others:
                copies.append(
                    pltpu.make_async_remote_copy(
                        src_ref=stage.at[half, pl.ds(first, count)],
                        dst_ref=far.at[half - 1, k, pl.ds(0, count)],
                        send_sem=send_sem.at[half, k + 1], recv_sem=recv_sem.at[half, k + 1],
                        device_id=(where_d, other_az(k + 1, -1)), device_id_type=MESH,
                    )
                )
        return copies

    def up_copies(half):
        return halo_copies(half, up_stage, halo_below, far_below, up_send, up_recv, me_d + 1)

    def down_copies(half):
        return halo_copies(half, down_stage, halo_above, far_above, down_send, down_recv, me_d - 1)

    stress_dz = [(s_rest, 2), (s_az, 2), (s_rest, 1), (s_az, 3)]
    vel_dz = [(v_az, 0), (v_az, 1), (v_az, 2), (v_rest, 1)]

    def top_of(read, base):
        return weighted([(stencil[4, l], read(base + l)) for l in range(4)])

    def bottom_of(read):
        return weighted([(stencil[0, l] * (2.0 if l == 0 else 1.0), read(l)) for l in range(5)])

    def reader(ref, k):
        return lambda z: ref[k, z]

    def far_reader(ref, k, f):
        return lambda z: ref[k, f, z]

    def send_down(half, dz_fields):
        for f, (ref, k) in enumerate(dz_fields):
            down_stage[half, f] = ref[k, 0]

        @pl.when(has_down)
        def _():
            for copy in down_copies(half):
                copy.start()

    def send_up(half, dz_fields):
        for f, (ref, k) in enumerate(dz_fields):
            up_stage[half, f] = top_of(reader(ref, k), depth - 4)

        @pl.when(has_up)
        def _():
            for copy in up_copies(half):
                copy.start()

    def receive_halos(half, dz_fields):
        for e in range(1, chunks):
            for f, (ref, k) in enumerate(dz_fields):
                partial[f, e] = top_of(reader(ref, k), 4 * (e - 1))

        @pl.when(has_up)
        def _():
            down_copies(half)[0].wait_recv()
            for f, (ref, k) in enumerate(dz_fields):
                ref[k, depth] = halo_above[half, f]

        @pl.when(jnp.logical_not(has_up))
        def _():
            for f, (ref, k) in enumerate(dz_fields):
                ref[k, depth] = jnp.zeros((azims, radii), F32)

        @pl.when(has_down)
        def _():
            up_copies(half)[0].wait_recv()
            partial[:, 0] = halo_below[half]

        @pl.when(jnp.logical_not(has_down))
        def _():
            for f, (ref, k) in enumerate(dz_fields):
                partial[f, 0] = bottom_of(reader(ref, k))

    def far_list(half):
        return [(k, i, f) for k in others for i, f in enumerate(FAR_DZ[half])]

    def far_partials(half, ref, e):
        for k, i, f in far_list(half):
            far_partial[k, i, e] = top_of(far_reader(ref, k, f), 4 * (e - 1))

    def receive_far_top(half, ref):
        @pl.when(has_up)
        def _():
            for copy in down_copies(half)[1:]:
                copy.wait_recv()
            for k, i, f in far_list(half):
                ref[k, f, depth] = far_above[half - 1, k, i]

        @pl.when(jnp.logical_not(has_up))
        def _():
            for k, i, f in far_list(half):
                ref[k, f, depth] = jnp.zeros((azims, radii), F32)

    def receive_far_bottom(half, ref):
        @pl.when(has_down)
        def _():
            for copy in up_copies(half)[1:]:
                copy.wait_recv()
            for k, i, f in far_list(half):
                far_partial[k, i, 0] = far_below[half - 1, k, i]

        @pl.when(jnp.logical_not(has_down))
        def _():
            for k, i, f in far_list(half):
                far_partial[k, i, 0] = bottom_of(far_reader(ref, k, f))

    def finish_az(which):
        for e in range(chunks):
            for copy in az_copies(which, e):
                copy.wait_send()

    def finish_halos(half):
        @pl.when(has_up)
        def _():
            for copy in up_copies(half):
                copy.wait_send()

        @pl.when(has_down)
        def _():
            for copy in down_copies(half):
                copy.wait_send()

    def dz_at(read, below, base, j):
        if j == 0:
            total = weighted([(stencil[0, l], read(base + l)) for l in range(1, 5)])
            return (total + below) * np.float32(1.0 / (2.0 * weights[0]))
        return weighted([(2.0 * derivative[j, l], read(base + l)) for l in range(5)])

    def high_low(value, axis):
        high = value.astype(BF16)
        low = (value - high.astype(F32)).astype(BF16)
        return jnp.concatenate([high, low, high], axis=axis)

    def radial_part(blocks):
        rows = jnp.concatenate([block.reshape(4 * azims, radii) for block in blocks], axis=0)
        result = jnp.dot(high_low(rows, 1), radial_k[...], preferred_element_type=F32)
        rad_d[0 : len(blocks)] = result.reshape(len(blocks), 4, azims, radii)

    def azimuth_part(near, far, base, kept):
        rows = azims * az_devices if kept else azims
        for j in range(4):
            blocks = [jnp.concatenate([ref[f, base + j] for ref, f in near], axis=1)]
            for k in others:
                blocks.append(jnp.concatenate([ref[k, f, base + j] for ref, f in far], axis=1))
            column = jnp.concatenate(blocks, axis=0)
            result = jnp.dot(
                azim_k[0:rows, :], high_low(column, 0), preferred_element_type=F32
            )
            az_d[j] = result[0:azims]
            for i, f in enumerate(kept):
                for k in others:
                    far_dt[k, i, base + j] = result[
                        (k + 1) * azims : (k + 2) * azims, f * radii : (f + 1) * radii
                    ]

    def az_at(j, f):
        return az_d[j, :, f * radii : (f + 1) * radii]

    def row_of(e):
        def row(index):
            return coef[index, pl.ds(e, 1), :]

        return row

    def shot_at(step, z):
        gain = np.float32(DT * SOURCE_GAIN * math.cos(0.9 * step))
        lane = lax.broadcasted_iota(jnp.int32, (1, radii), 1)
        wanted = jnp.zeros((1, radii), jnp.int32) + source[0]
        return jnp.where((wanted == me_d * depth + z) & (lane < 4 * RB), gain, np.float32(0.0))

    def velocity_chunk(step, e):
        base = pl.multiple_of(4 * e, 4)
        planes = pl.ds(base, 4)
        row = row_of(e)
        if step == 0:
            receive_az(0, e)
        else:
            receive_az(3, e)
            for k in others:
                for j in range(4):
                    z = base + j
                    far_s[k, 1, z] = far_s[k, 1, z] + row(BM) * far_dw[k, 0, z]
                    far_s[k, 3, z] = far_s[k, 3, z] - row(PM) * far_dw[k, 0, z]
        radial_part([s_rest[0, planes], s_az[0, planes], s_rest[2, planes], s_az[3, planes]])
        azimuth_part(
            [(s_az, f) for f in range(4)], [(far_s, f) for f in range(4)], base,
            (1, 3) if step == 1 else (),
        )
        q = inv_r[...]
        for j in range(4):
            z = base + j
            rt, tt = s_az[0, z], s_az[1, z]
            rr, rz = s_rest[0, z], s_rest[2, z]
            dz = [
                dz_at(reader(ref, k), partial[f, e], base, j)
                for f, (ref, k) in enumerate(stress_dz)
            ]
            div = [
                rad_d[0, j] + q * (az_at(j, 0) + (rr - tt)) + dz[0],
                rad_d[1, j] + q * (az_at(j, 1) + 2.0 * rt) + dz[1],
                rad_d[2, j] + q * (az_at(j, 2) + rz) + dz[2],
            ]
            grad = [rad_d[3, j], q * az_at(j, 3), dz[3]]
            solid = [(v_az, 0), (v_az, 2), (v_az, 1)]
            fluid = [(v_rest, 0), (v_az, 3), (v_rest, 1)]
            for c in range(3):
                psi = [mem[3 * pole + c, z] for pole in range(4)]
                resist = grad[c]
                for pole in range(4):
                    resist = resist + row(FA + pole) * psi[pole]
                ref, k = solid[c]
                ref[k, z] = ref[k, z] + (row(A1) * div[c] + row(A2) * resist)
                change = -(row(A2) * div[c] + row(A3) * resist)
                ref, k = fluid[c]
                fresh = ref[k, z] + change
                ref[k, z] = fresh
                change = change + row(OM) * fresh
                psi = [(psi[pole] + change) * row(INV + pole) for pole in range(4)]
                for pole in range(4):
                    mem[3 * pole + c, z] = psi[pole]
                if c == 1 and step == 0:
                    total = row(FA) * psi[0]
                    for pole in range(1, 4):
                        total = total + row(FA + pole) * psi[pole]
                    psi_t[0, z] = total

    def stress_chunk(step, e):
        base = pl.multiple_of(4 * e, 4)
        planes = pl.ds(base, 4)
        radial_part([v_az[0, planes], v_az[2, planes], v_az[1, planes], v_rest[0, planes]])
        if step == 0:
            receive_az(1, e)
            far = [(far_v, f) for f in range(4)]
        else:
            receive_az(4, e)
            far = [(far_new, 0), (far_new, 1), (far_v, 2), (far_v, 3)]
        azimuth_part([(v_az, f) for f in range(4)], far, base, (0, 1, 2) if step == 0 else ())
        row = row_of(e)
        q = inv_r[...]
        for j in range(4):
            z = base + j
            vr, vt, wr = v_az[0, z], v_az[2, z], v_rest[0, z]
            dz = [
                dz_at(reader(ref, k), partial[f, e], base, j)
                for f, (ref, k) in enumerate(vel_dz)
            ]
            e_rr = rad_d[0, j]
            e_tt = q * (vr + az_at(j, 2))
            e_zz = dz[1]
            g_rt = q * (az_at(j, 0) - vt) + rad_d[1, j]
            g_rz = dz[0] + rad_d[2, j]
            g_tz = dz[2] + q * az_at(j, 1)
            div_v = e_rr + e_tt + e_zz
            div_w = rad_d[3, j] + q * (wr + az_at(j, 3)) + dz[3]
            if step == 0:
                dw[0, z] = div_w
            bulk = row(LF) * div_v + row(BM) * div_w
            twice = 2.0 * row(MU)
            s_rest[0, z] = s_rest[0, z] + (bulk + twice * e_rr)
            s_az[1, z] = s_az[1, z] + (bulk + twice * e_tt)
            s_rest[1, z] = s_rest[1, z] + (bulk + twice * e_zz)
            s_az[0, z] = s_az[0, z] + row(MU) * g_rt
            s_rest[2, z] = s_rest[2, z] + row(MU) * g_rz
            s_az[2, z] = s_az[2, z] + row(MU) * g_tz
            s_az[3, z] = s_az[3, z] - (row(BM) * div_v + row(PM) * div_w) + shot_at(step, z)

    def far_stress_chunk(e):
        base = pl.multiple_of(4 * e, 4)
        planes = pl.ds(base, 4)
        row = row_of(e)
        q = inv_r[...]
        for k in others:
            radial_part([far_v[k, 0, planes], far_v[k, 2, planes]])
            for j in range(4):
                z = base + j
                vr, vt = far_v[k, 0, z], far_v[k, 2, z]
                dz_vz = dz_at(far_reader(far_v, k, 1), far_partial[k, 0, e], base, j)
                dz_vt = dz_at(far_reader(far_v, k, 2), far_partial[k, 1, e], base, j)
                e_tt = q * (vr + far_dt[k, 2, z])
                div_v = rad_d[0, j] + e_tt + dz_vz
                g_rt = q * (far_dt[k, 0, z] - vt) + rad_d[1, j]
                g_tz = dz_vt + q * far_dt[k, 1, z]
                far_s[k, 0, z] = far_s[k, 0, z] + row(MU) * g_rt
                far_s[k, 1, z] = far_s[k, 1, z] + (row(LF) * div_v + 2.0 * row(MU) * e_tt)
                far_s[k, 2, z] = far_s[k, 2, z] + row(MU) * g_tz
                far_s[k, 3, z] = far_s[k, 3, z] - row(BM) * div_v + shot_at(0, z)

    def far_velocity_chunk(e):
        base = pl.multiple_of(4 * e, 4)
        planes = pl.ds(base, 4)
        row = row_of(e)
        q = inv_r[...]
        receive_az(2, e)
        for k in others:
            radial_part([far_s[k, 0, planes]])
            for j in range(4):
                z = base + j
                dz_tz = dz_at(far_reader(far_s, k, 2), far_partial[k, 0, e], base, j)
                div = rad_d[0, j] + q * (far_dt[k, 0, z] + 2.0 * far_s[k, 0, z]) + dz_tz
                resist = q * far_dt[k, 1, z] + far_psi[k, 0, z]
                far_v[k, 2, z] = far_v[k, 2, z] + (row(A1) * div + row(A2) * resist)
                far_v[k, 3, z] = far_v[k, 3, z] - (row(A2) * div + row(A3) * resist)

    def each_chunk(body):
        def wrapped(e, carry):
            body(e)
            return carry

        lax.fori_loop(0, chunks, wrapped, 0)

    for index in (1, 3, 5, 6):
        loads[index].wait()
    order = [0] + ([chunks - 1] if chunks > 1 else []) + list(range(1, chunks - 1))
    for e in order:
        start_az(0, e)
    for index in (0, 2, 4):
        loads[index].wait()
    send_down(0, stress_dz)
    send_up(0, stress_dz)
    for index in range(14, 19):
        loads[index].wait()

    elements = ids.shape[1]
    spread = lax.broadcasted_iota(jnp.int32, (elements, radii), 0) == (
        lax.broadcasted_iota(jnp.int32, (elements, radii), 1) >> 2
    )
    ids_node = jnp.dot(
        ids[...].astype(F32).astype(BF16), spread.astype(F32).astype(BF16),
        preferred_element_type=F32,
    )
    node = lax.broadcasted_iota(jnp.int32, (1, radii), 1)
    place = node & 3
    inside = jnp.zeros((1, radii), F32)
    for j in range(1, 4):
        inside = jnp.where(place == j, np.float32(0.5 * (1.0 + gll_nodes[j])), inside)
    inv_r[...] = 1.0 / (np.float32(R_INNER) + (node >> 2).astype(F32) + inside)

    def pick(table, column):
        value = jnp.zeros_like(ids_node)
        for r in range(8):
            value = jnp.where(ids_node == float(r), table[r : r + 1, column : column + 1], value)
        return value

    lame_zero, shear, modulus, coupling, rho, rho_f, tort, fric = [pick(mats, c) for c in range(8)]
    omega = pick(jkd, 0)
    rho_w = rho_f * tort
    scale = DT / (rho * rho_w - rho_f * rho_f)
    coef[A1] = rho_w * scale
    coef[A2] = rho_f * scale
    coef[A3] = rho * scale
    for pole in range(4):
        coef[FA + pole] = fric * pick(jkd, 1 + pole)
        coef[INV + pole] = 1.0 / (1.0 + DT * (pick(jkd, 5 + pole) + omega))
    coef[OM] = DT * omega
    coef[LF] = DT * (lame_zero + coupling * coupling * modulus)
    coef[BM] = DT * coupling * modulus
    coef[MU] = DT * shear
    coef[PM] = DT * modulus

    for index in range(7, 14):
        loads[index].wait()

    stores = []

    def to_out(src, dst):
        copy = pltpu.make_async_copy(src, dst, store_sem.at[len(stores)])
        copy.start()
        stores.append(copy)

    receive_halos(0, stress_dz)

    def first_velocity(turn):
        last = chunks - 1
        e = jnp.where(turn == 0, 0, jnp.where(turn == 1, last, turn - 1))
        velocity_chunk(0, e)

        @pl.when(turn == 0)
        def _():
            send_down(1, vel_dz)

        @pl.when(turn == min(1, last))
        def _():
            send_up(1, vel_dz)

        @pl.when((turn != 1) | (last == 1))
        def _():
            start_az(1, e)

        @pl.when((turn == last) & (last > 1))
        def _():
            start_az(1, last)

    each_chunk(first_velocity)
    for e in range(chunks):
        start_az(2, e)
    finish_az(0)
    finish_halos(0)

    receive_halos(1, vel_dz)

    def first_stress(e):
        stress_chunk(0, e)
        start_az(3, e)

        @pl.when(e == 0)
        def _():
            send_down(2, stress_dz)

        @pl.when(e == chunks - 1)
        def _():
            send_up(2, stress_dz)
            receive_far_top(1, far_v)

        @pl.when(e == 1)
        def _():
            receive_far_bottom(1, far_v)

        @pl.when(e > 0)
        def _():
            far_partials(1, far_v, e)
            far_stress_chunk(e - 1)

    each_chunk(first_stress)
    far_stress_chunk(chunks - 1)
    finish_az(1)
    finish_halos(1)

    receive_halos(2, stress_dz)

    def second_velocity(e):
        velocity_chunk(1, e)
        start_az(4, e)

        @pl.when(e == 0)
        def _():
            send_down(3, vel_dz)

    each_chunk(second_velocity)
    send_up(3, vel_dz)
    for i, (ref, k) in enumerate(vel_place):
        to_out(ref.at[k, inner], vel_out.at[i])
    to_out(mem, mem_out)
    receive_far_top(2, far_s)
    receive_far_bottom(2, far_s)
    for e in range(1, chunks):
        far_partials(2, far_s, e)
    each_chunk(far_velocity_chunk)
    finish_az(2)
    finish_az(3)
    finish_halos(2)

    receive_halos(3, vel_dz)

    def chunk_stores(e):
        planes = pl.ds(pl.multiple_of(4 * e, 4), 4)
        return [
            pltpu.make_async_copy(ref.at[k, planes], str_out.at[i, planes], chunk_sem.at[e, i])
            for i, (ref, k) in enumerate(stress_place)
        ]

    def second_stress(e):
        stress_chunk(1, e)
        for copy in chunk_stores(e):
            copy.start()

    each_chunk(second_stress)
    finish_az(4)
    finish_halos(3)
    for copy in stores:
        copy.wait()
    for e in range(chunks):
        for copy in chunk_stores(e):
            copy.wait()


FAR_DZ = {1: (1, 2), 2: (2,)}


def on_device(depth_devices, az_devices, velocity, stress, memory, layer_ids, materials, jkd, source_depth):
    depth, azims, radii = velocity.shape[1:]
    chunks = depth // 4
    halves = 2 * STEPS
    others = max(az_devices - 1, 1)
    azim_total = azims * az_devices
    radial_high, radial_low = split_high_low(radial_operator(radii).T)
    radial_k = np.concatenate([radial_high, radial_high, radial_low], axis=0)
    azim_high, azim_low = split_high_low(azimuth_operator(azim_total))
    azim_k = np.concatenate([azim_high, azim_high, azim_low], axis=1)
    plane = (azims, radii)
    smem = pl.BlockSpec(memory_space=pltpu.SMEM)
    hbm = pl.BlockSpec(memory_space=pltpu.HBM)
    dma = pltpu.SemaphoreType.DMA
    constants = [radial_k, azim_k]
    small = [materials, jkd, layer_ids] + [jnp.asarray(value) for value in constants]

    def held(*shape):
        return pltpu.VMEM(shape + plane, F32)

    return tuple(pl.pallas_call(
        functools.partial(step_kernel, depth_devices, az_devices),
        out_shape=tuple(jax.ShapeDtypeStruct(x.shape, x.dtype) for x in (velocity, stress, memory)),
        in_specs=[smem] + [hbm] * 8,
        out_specs=(hbm, hbm, hbm),
        scratch_shapes=[pltpu.VMEM(value.shape, value.dtype) for value in small] + [
            held(12, depth),
            pltpu.VMEM((1, radii), F32),
            held(4, depth + 1),
            held(3, depth + 1),
            held(4, depth + 1),
            held(2, depth + 1),
            held(others, 4, depth + 1),
            held(others, 4, depth + 1),
            held(others, 2, depth),
            held(others, 1, depth),
            held(others, 1, depth),
            held(others, 3, depth),
            held(1, depth),
            held(1, depth),
            held(halves, 4),
            held(halves, 4),
            held(2, others, 2),
            held(2, others, 2),
            held(halves, 4),
            held(halves, 4),
            held(4, chunks),
            held(others, 2, chunks),
            pltpu.VMEM((NCOEF, chunks, radii), F32),
            held(4, 4),
            pltpu.VMEM((4, azims, 4 * radii), F32),
            dma((19,)),
            dma((7,)),
            dma((chunks, 7)),
            dma((5, others, chunks)),
            dma((5, others, chunks)),
            dma((halves, others + 1)),
            dma((halves, others + 1)),
            dma((halves, others + 1)),
            dma((halves, others + 1)),
        ],
        compiler_params=pltpu.CompilerParams(
            collective_id=0, has_side_effects=True, vmem_limit_bytes=64 * 1024 * 1024
        ),
        cost_estimate=pl.CostEstimate(
            flops=10**9, bytes_accessed=2 * 25 * velocity.size // 6 * 4, transcendentals=0
        ),
        name="biot_steps",
    )(source_depth, *small, velocity, stress, memory))


def solution(mesh):
    return jax.shard_map(
        functools.partial(on_device, mesh.shape["depth"], mesh.shape["az"]),
        mesh=mesh,
        in_specs=(
            P(None, "depth", "az", None),
            P(None, "depth", "az", None),
            P(None, "depth", "az", None),
            P("depth", None),
            P(),
            P(),
            P(),
        ),
        out_specs=(
            P(None, "depth", "az", None),
            P(None, "depth", "az", None),
            P(None, "depth", "az", None),
        ),
        check_vma=False,
    )
```

```python
import functools
import math

import jax
import jax.numpy as jnp
import numpy as np
from jax import lax
from jax.experimental import pallas as pl
from jax.experimental.pallas import tpu as pltpu
from jax.sharding import PartitionSpec as P

STEPS = 2
RB = 4


DT = 0.02
SOURCE_GAIN = 40.0
R_INNER = 1.0
MESH = pl.DeviceIdType.MESH
F32 = jnp.float32
BF16 = jnp.bfloat16


def gll_basis():
    root_value = math.sqrt(3.0 / 7.0)
    gll_nodes = np.array([-1.0, -root_value, 0.0, root_value, 1.0])
    weights = np.array([0.1, 49.0 / 90.0, 32.0 / 45.0, 49.0 / 90.0, 0.1])
    offsets = gll_nodes[:, None] - gll_nodes[None, :] + np.eye(5)
    factors = np.prod(offsets, axis=1)
    derivative = factors[:, None] / factors[None, :] / offsets
    diagonal_part = np.sum(1.0 / offsets, axis=1) - 1.0
    derivative = derivative * (1.0 - np.eye(5)) + np.eye(5) * diagonal_part[:, None]
    return (gll_nodes, weights, derivative)


def radial_operator(node_count):
    gll_nodes, weights, derivative = gll_basis()
    full_count = node_count + 1
    stencil = weights[:, None] * derivative * 2.0
    assembled = np.zeros((full_count, full_count))
    node_mass = np.zeros(full_count)
    for element in range(node_count // 4):
        assembled[4 * element : 4 * element + 5, 4 * element : 4 * element + 5] += stencil
        node_mass[4 * element : 4 * element + 5] += weights
    return (assembled / node_mass[:, None])[:node_count, :node_count]


def azimuth_operator(node_count):
    positions = np.arange(node_count)
    offsets = positions[:, None] - positions[None, :]
    wave_modes = np.arange(1, node_count // 2)
    phases = 2.0 * np.pi * offsets[:, :, None] * wave_modes[None, None, :] / node_count
    return -(2.0 / node_count) * np.sum(wave_modes * np.sin(phases), axis=2)


def split_high_low(matrix):
    matrix = np.asarray(matrix, np.float32)
    high = matrix.astype(jnp.bfloat16)
    low = (matrix - high.astype(np.float32)).astype(jnp.bfloat16)
    return high, low


A1, A2, A3, FA, OM, INV, LF, BM, MU, PM, NCOEF = 0, 1, 2, 3, 7, 8, 12, 13, 14, 15, 16


def weighted(terms):
    total = None
    for factor, value in terms:
        if abs(factor) < 1e-12:
            continue
        term = value * np.float32(factor)
        total = term if total is None else total + term
    return total


def step_kernel(
    depth_devices, az_devices,
    source, mats_in, jkd_in, ids_in, radial_in, azim_in, vel_in, str_in, mem_in,
    coef_out, inv_r_out, partial_out, sa_out, sr_out, va_out, vr_out, fv_out, far_new, mem_out,
    mats, jkd, ids, radial_k, azim_k,
    mem, inv_r, s_az, s_rest, v_az, v_rest, far_s, far_v, far_dw, far_psi, far_dt, dw, psi_t,
    halo_above, halo_below, far_above, far_below, up_stage, down_stage,
    partial, far_partial, coef, rad_d, az_d,
    load_sem, first_sem, store_sem, az_send, az_recv, up_send, up_recv, down_send, down_recv,
):
    me_d = lax.axis_index("depth")
    me_a = lax.axis_index("az")
    depth, azims, radii = mem.shape[1:]
    chunks = depth // 4
    others = range(az_devices - 1)
    has_up = me_d < depth_devices - 1
    has_down = me_d > 0
    gll_nodes, weights, derivative = gll_basis()
    stencil = weights[:, None] * derivative * 2.0

    inner = pl.ds(0, depth)
    stress_place = [(s_rest, 0), (s_az, 1), (s_rest, 1), (s_az, 0), (s_rest, 2), (s_az, 2), (s_az, 3)]
    vel_place = [(v_az, 0), (v_az, 2), (v_az, 1), (v_rest, 0), (v_az, 3), (v_rest, 1)]
    pairs = [(str_in.at[i], ref.at[k, inner]) for i, (ref, k) in enumerate(stress_place)]
    pairs += [(vel_in.at[i], ref.at[k, inner]) for i, (ref, k) in enumerate(vel_place)]
    pairs += [(mem_in, mem), (mats_in, mats), (jkd_in, jkd), (ids_in, ids)]
    pairs += [(radial_in, radial_k), (azim_in, azim_k)]
    loads = [
        pltpu.make_async_copy(src, dst, load_sem.at[i]) for i, (src, dst) in enumerate(pairs)
    ]
    order = [0] + ([chunks - 1] if chunks > 1 else []) + list(range(1, chunks - 1))

    def first_loads(e):
        planes = pl.ds(4 * e, 4)
        return [
            pltpu.make_async_copy(
                str_in.at[i, planes], s_az.at[k, planes], first_sem.at[e, k]
            )
            for k, i in enumerate((3, 1, 5, 6))
        ]

    for e in order:
        for copy in first_loads(e):
            copy.start()
    for index in (14, 15, 16, 0, 2, 4, 17, 18, 7, 8, 9, 10, 11, 12, 13):
        loads[index].start()

    def other_az(k, sign):
        return lax.rem(me_a + (az_devices + sign * k), az_devices)

    barrier = pltpu.get_barrier_semaphore()

    def greet(where_d, where_a):
        pl.semaphore_signal(barrier, inc=1, device_id=(where_d, where_a), device_id_type=MESH)

    for k in range(1, az_devices):
        greet(me_d, other_az(k, 1))

    @pl.when(has_up)
    def _():
        for k in range(az_devices):
            greet(me_d + 1, other_az(k, 1))

    @pl.when(has_down)
    def _():
        for k in range(az_devices):
            greet(me_d - 1, other_az(k, 1))

    neighbours = has_up.astype(jnp.int32) + has_down.astype(jnp.int32)
    pl.semaphore_wait(barrier, (az_devices - 1) + az_devices * neighbours)

    exchanges = [
        (s_az, far_s, 4), (v_az, far_v, 4), (psi_t, far_psi, 1), (dw, far_dw, 1), (v_az, far_new, 2),
    ]

    def az_copies(which, e):
        source_ref, target_ref, count = exchanges[which]
        planes = pl.ds(pl.multiple_of(4 * e, 4), 4)
        return [
            pltpu.make_async_remote_copy(
                src_ref=source_ref.at[pl.ds(0, count), planes],
                dst_ref=target_ref.at[k, pl.ds(0, count), planes],
                send_sem=az_send.at[which, k, e],
                recv_sem=az_recv.at[which, k, e],
                device_id=(me_d, other_az(k + 1, -1)),
                device_id_type=MESH,
            )
            for k in others
        ]

    def start_az(which, e):
        for copy in az_copies(which, e):
            copy.start()

    def receive_az(which, e):
        for copy in az_copies(which, e):
            copy.wait_recv()

    far_fields = {1: (1, 2), 2: (1, 1)}

    def halo_copies(half, stage, near, far, send_sem, recv_sem, where_d):
        copies = [
            pltpu.make_async_remote_copy(
                src_ref=stage.at[half], dst_ref=near.at[half],
                send_sem=send_sem.at[half, 0], recv_sem=recv_sem.at[half, 0],
                device_id=(where_d, me_a), device_id_type=MESH,
            )
        ]
        if half in far_fields:
            first, count = far_fields[half]
            for k in others:
                copies.append(
                    pltpu.make_async_remote_copy(
                        src_ref=stage.at[half, pl.ds(first, count)],
                        dst_ref=far.at[half - 1, k, pl.ds(0, count)],
                        send_sem=send_sem.at[half, k + 1], recv_sem=recv_sem.at[half, k + 1],
                        device_id=(where_d, other_az(k + 1, -1)), device_id_type=MESH,
                    )
                )
        return copies

    def up_copies(half):
        return halo_copies(half, up_stage, halo_below, far_below, up_send, up_recv, me_d + 1)

    def down_copies(half):
        return halo_copies(half, down_stage, halo_above, far_above, down_send, down_recv, me_d - 1)

    stress_dz = [(s_rest, 2), (s_az, 2), (s_rest, 1), (s_az, 3)]
    vel_dz = [(v_az, 0), (v_az, 1), (v_az, 2), (v_rest, 1)]

    def top_of(read, base):
        return weighted([(stencil[4, l], read(base + l)) for l in range(4)])

    def bottom_of(read):
        return weighted([(stencil[0, l] * (2.0 if l == 0 else 1.0), read(l)) for l in range(5)])

    def reader(ref, k):
        return lambda z: ref[k, z]

    def far_reader(ref, k, f):
        return lambda z: ref[k, f, z]

    def send_down(half, dz_fields):
        for f, (ref, k) in enumerate(dz_fields):
            down_stage[half, f] = ref[k, 0]

        @pl.when(has_down)
        def _():
            for copy in down_copies(half):
                copy.start()

    def send_up(half, dz_fields):
        for f, (ref, k) in enumerate(dz_fields):
            up_stage[half, f] = top_of(reader(ref, k), depth - 4)

        @pl.when(has_up)
        def _():
            for copy in up_copies(half):
                copy.start()

    def receive_halos(half, dz_fields):
        for e in range(1, chunks):
            for f, (ref, k) in enumerate(dz_fields):
                partial[f, e] = top_of(reader(ref, k), 4 * (e - 1))

        @pl.when(has_up)
        def _():
            down_copies(half)[0].wait_recv()
            for f, (ref, k) in enumerate(dz_fields):
                ref[k, depth] = halo_above[half, f]

        @pl.when(jnp.logical_not(has_up))
        def _():
            for f, (ref, k) in enumerate(dz_fields):
                ref[k, depth] = jnp.zeros((azims, radii), F32)

        @pl.when(has_down)
        def _():
            up_copies(half)[0].wait_recv()
            partial[:, 0] = halo_below[half]

        @pl.when(jnp.logical_not(has_down))
        def _():
            for f, (ref, k) in enumerate(dz_fields):
                partial[f, 0] = bottom_of(reader(ref, k))

    def far_list(half):
        return [(k, i, f) for k in others for i, f in enumerate(FAR_DZ[half])]

    def far_partials(half, ref, e):
        for k, i, f in far_list(half):
            far_partial[k, i, e] = top_of(far_reader(ref, k, f), 4 * (e - 1))

    def receive_far_top(half, ref):
        @pl.when(has_up)
        def _():
            for copy in down_copies(half)[1:]:
                copy.wait_recv()
            for k, i, f in far_list(half):
                ref[k, f, depth] = far_above[half - 1, k, i]

        @pl.when(jnp.logical_not(has_up))
        def _():
            for k, i, f in far_list(half):
                ref[k, f, depth] = jnp.zeros((azims, radii), F32)

    def receive_far_bottom(half, ref):
        @pl.when(has_down)
        def _():
            for copy in up_copies(half)[1:]:
                copy.wait_recv()
            for k, i, f in far_list(half):
                far_partial[k, i, 0] = far_below[half - 1, k, i]

        @pl.when(jnp.logical_not(has_down))
        def _():
            for k, i, f in far_list(half):
                far_partial[k, i, 0] = bottom_of(far_reader(ref, k, f))

    def finish_az(which):
        for e in range(chunks):
            for copy in az_copies(which, e):
                copy.wait_send()

    def finish_halos(half):
        @pl.when(has_up)
        def _():
            for copy in up_copies(half):
                copy.wait_send()

        @pl.when(has_down)
        def _():
            for copy in down_copies(half):
                copy.wait_send()

    def dz_at(read, below, base, j):
        if j == 0:
            total = weighted([(stencil[0, l], read(base + l)) for l in range(1, 5)])
            return (total + below) * np.float32(1.0 / (2.0 * weights[0]))
        return weighted([(2.0 * derivative[j, l], read(base + l)) for l in range(5)])

    def high_low(value, axis):
        high = value.astype(BF16)
        low = (value - high.astype(F32)).astype(BF16)
        return jnp.concatenate([high, low, high], axis=axis)

    def radial_part(blocks):
        rows = jnp.concatenate([block.reshape(4 * azims, radii) for block in blocks], axis=0)
        result = jnp.dot(high_low(rows, 1), radial_k[...], preferred_element_type=F32)
        rad_d[0 : len(blocks)] = result.reshape(len(blocks), 4, azims, radii)

    def azimuth_part(near, far, base, kept):
        rows = azims * az_devices if kept else azims
        for j in range(4):
            blocks = [jnp.concatenate([ref[f, base + j] for ref, f in near], axis=1)]
            for k in others:
                blocks.append(jnp.concatenate([ref[k, f, base + j] for ref, f in far], axis=1))
            column = jnp.concatenate(blocks, axis=0)
            result = jnp.dot(
                azim_k[0:rows, :], high_low(column, 0), preferred_element_type=F32
            )
            az_d[j] = result[0:azims]
            for i, f in enumerate(kept):
                for k in others:
                    far_dt[k, i, base + j] = result[
                        (k + 1) * azims : (k + 2) * azims, f * radii : (f + 1) * radii
                    ]

    def az_at(j, f):
        return az_d[j, :, f * radii : (f + 1) * radii]

    def row_of(e):
        def row(index):
            return coef[index, pl.ds(e, 1), :]

        return row

    def shot_at(step, z):
        gain = np.float32(DT * SOURCE_GAIN * math.cos(0.9 * step))
        lane = lax.broadcasted_iota(jnp.int32, (1, radii), 1)
        wanted = jnp.zeros((1, radii), jnp.int32) + source[0]
        return jnp.where((wanted == me_d * depth + z) & (lane < 4 * RB), gain, np.float32(0.0))

    def velocity_chunk(step, e):
        base = pl.multiple_of(4 * e, 4)
        planes = pl.ds(base, 4)
        row = row_of(e)
        if step == 0:
            receive_az(0, e)
        else:
            receive_az(3, e)
            for k in others:
                for j in range(4):
                    z = base + j
                    far_s[k, 1, z] = far_s[k, 1, z] + row(BM) * far_dw[k, 0, z]
                    far_s[k, 3, z] = far_s[k, 3, z] - row(PM) * far_dw[k, 0, z]
        radial_part([s_rest[0, planes], s_az[0, planes], s_rest[2, planes], s_az[3, planes]])
        azimuth_part(
            [(s_az, f) for f in range(4)], [(far_s, f) for f in range(4)], base,
            (1, 3) if step == 1 else (),
        )
        q = inv_r[...]
        for j in range(4):
            z = base + j
            rt, tt = s_az[0, z], s_az[1, z]
            rr, rz = s_rest[0, z], s_rest[2, z]
            dz = [
                dz_at(reader(ref, k), partial[f, e], base, j)
                for f, (ref, k) in enumerate(stress_dz)
            ]
            div = [
                rad_d[0, j] + q * (az_at(j, 0) + (rr - tt)) + dz[0],
                rad_d[1, j] + q * (az_at(j, 1) + 2.0 * rt) + dz[1],
                rad_d[2, j] + q * (az_at(j, 2) + rz) + dz[2],
            ]
            grad = [rad_d[3, j], q * az_at(j, 3), dz[3]]
            solid = [(v_az, 0), (v_az, 2), (v_az, 1)]
            fluid = [(v_rest, 0), (v_az, 3), (v_rest, 1)]
            for c in range(3):
                psi = [mem[3 * pole + c, z] for pole in range(4)]
                resist = grad[c]
                for pole in range(4):
                    resist = resist + row(FA + pole) * psi[pole]
                ref, k = solid[c]
                ref[k, z] = ref[k, z] + (row(A1) * div[c] + row(A2) * resist)
                change = -(row(A2) * div[c] + row(A3) * resist)
                ref, k = fluid[c]
                fresh = ref[k, z] + change
                ref[k, z] = fresh
                change = change + row(OM) * fresh
                psi = [(psi[pole] + change) * row(INV + pole) for pole in range(4)]
                for pole in range(4):
                    mem[3 * pole + c, z] = psi[pole]
                if c == 1 and step == 0:
                    total = row(FA) * psi[0]
                    for pole in range(1, 4):
                        total = total + row(FA + pole) * psi[pole]
                    psi_t[0, z] = total

    def stress_chunk(step, e):
        base = pl.multiple_of(4 * e, 4)
        planes = pl.ds(base, 4)
        radial_part([v_az[0, planes], v_az[2, planes], v_az[1, planes], v_rest[0, planes]])
        receive_az(1, e)
        far = [(far_v, f) for f in range(4)]
        azimuth_part([(v_az, f) for f in range(4)], far, base, (0, 1, 2))
        row = row_of(e)
        q = inv_r[...]
        for j in range(4):
            z = base + j
            vr, vt, wr = v_az[0, z], v_az[2, z], v_rest[0, z]
            dz = [
                dz_at(reader(ref, k), partial[f, e], base, j)
                for f, (ref, k) in enumerate(vel_dz)
            ]
            e_rr = rad_d[0, j]
            e_tt = q * (vr + az_at(j, 2))
            e_zz = dz[1]
            g_rt = q * (az_at(j, 0) - vt) + rad_d[1, j]
            g_rz = dz[0] + rad_d[2, j]
            g_tz = dz[2] + q * az_at(j, 1)
            div_v = e_rr + e_tt + e_zz
            div_w = rad_d[3, j] + q * (wr + az_at(j, 3)) + dz[3]
            if step == 0:
                dw[0, z] = div_w
            bulk = row(LF) * div_v + row(BM) * div_w
            twice = 2.0 * row(MU)
            s_rest[0, z] = s_rest[0, z] + (bulk + twice * e_rr)
            s_az[1, z] = s_az[1, z] + (bulk + twice * e_tt)
            s_rest[1, z] = s_rest[1, z] + (bulk + twice * e_zz)
            s_az[0, z] = s_az[0, z] + row(MU) * g_rt
            s_rest[2, z] = s_rest[2, z] + row(MU) * g_rz
            s_az[2, z] = s_az[2, z] + row(MU) * g_tz
            s_az[3, z] = s_az[3, z] - (row(BM) * div_v + row(PM) * div_w) + shot_at(step, z)

    def far_stress_chunk(e):
        base = pl.multiple_of(4 * e, 4)
        planes = pl.ds(base, 4)
        row = row_of(e)
        q = inv_r[...]
        for k in others:
            radial_part([far_v[k, 0, planes], far_v[k, 2, planes]])
            for j in range(4):
                z = base + j
                vr, vt = far_v[k, 0, z], far_v[k, 2, z]
                dz_vz = dz_at(far_reader(far_v, k, 1), far_partial[k, 0, e], base, j)
                dz_vt = dz_at(far_reader(far_v, k, 2), far_partial[k, 1, e], base, j)
                e_tt = q * (vr + far_dt[k, 2, z])
                div_v = rad_d[0, j] + e_tt + dz_vz
                g_rt = q * (far_dt[k, 0, z] - vt) + rad_d[1, j]
                g_tz = dz_vt + q * far_dt[k, 1, z]
                far_s[k, 0, z] = far_s[k, 0, z] + row(MU) * g_rt
                far_s[k, 1, z] = far_s[k, 1, z] + (row(LF) * div_v + 2.0 * row(MU) * e_tt)
                far_s[k, 2, z] = far_s[k, 2, z] + row(MU) * g_tz
                far_s[k, 3, z] = far_s[k, 3, z] - row(BM) * div_v + shot_at(0, z)

    def far_velocity_chunk(e):
        base = pl.multiple_of(4 * e, 4)
        planes = pl.ds(base, 4)
        row = row_of(e)
        q = inv_r[...]
        receive_az(2, e)
        for k in others:
            radial_part([far_s[k, 0, planes]])
            for j in range(4):
                z = base + j
                dz_tz = dz_at(far_reader(far_s, k, 2), far_partial[k, 0, e], base, j)
                div = rad_d[0, j] + q * (far_dt[k, 0, z] + 2.0 * far_s[k, 0, z]) + dz_tz
                resist = q * far_dt[k, 1, z] + far_psi[k, 0, z]
                far_v[k, 2, z] = far_v[k, 2, z] + (row(A1) * div + row(A2) * resist)
                far_v[k, 3, z] = far_v[k, 3, z] - (row(A2) * div + row(A3) * resist)

    def each_chunk(body):
        def wrapped(e, carry):
            body(e)
            return carry

        lax.fori_loop(0, chunks, wrapped, 0)

    for e in order:
        for copy in first_loads(e):
            copy.wait()
        start_az(0, e)
    for index in (0, 2, 4):
        loads[index].wait()
    send_down(0, stress_dz)
    send_up(0, stress_dz)
    for index in range(14, 19):
        loads[index].wait()

    elements = ids.shape[1]
    spread = lax.broadcasted_iota(jnp.int32, (elements, radii), 0) == (
        lax.broadcasted_iota(jnp.int32, (elements, radii), 1) >> 2
    )
    ids_node = jnp.dot(
        ids[...].astype(F32).astype(BF16), spread.astype(F32).astype(BF16),
        preferred_element_type=F32,
    )
    node = lax.broadcasted_iota(jnp.int32, (1, radii), 1)
    place = node & 3
    inside = jnp.zeros((1, radii), F32)
    for j in range(1, 4):
        inside = jnp.where(place == j, np.float32(0.5 * (1.0 + gll_nodes[j])), inside)
    inv_r[...] = 1.0 / (np.float32(R_INNER) + (node >> 2).astype(F32) + inside)

    def pick(table, column):
        value = jnp.zeros_like(ids_node)
        for r in range(8):
            value = jnp.where(ids_node == float(r), table[r : r + 1, column : column + 1], value)
        return value

    lame_zero, shear, modulus, coupling, rho, rho_f, tort, fric = [pick(mats, c) for c in range(8)]
    omega = pick(jkd, 0)
    rho_w = rho_f * tort
    scale = DT / (rho * rho_w - rho_f * rho_f)
    coef[A1] = rho_w * scale
    coef[A2] = rho_f * scale
    coef[A3] = rho * scale
    for pole in range(4):
        coef[FA + pole] = fric * pick(jkd, 1 + pole)
        coef[INV + pole] = 1.0 / (1.0 + DT * (pick(jkd, 5 + pole) + omega))
    coef[OM] = DT * omega
    coef[LF] = DT * (lame_zero + coupling * coupling * modulus)
    coef[BM] = DT * coupling * modulus
    coef[MU] = DT * shear
    coef[PM] = DT * modulus

    for index in range(7, 14):
        loads[index].wait()

    stores = []

    def to_out(src, dst):
        copy = pltpu.make_async_copy(src, dst, store_sem.at[len(stores)])
        copy.start()
        stores.append(copy)

    receive_halos(0, stress_dz)

    def first_velocity(turn):
        last = chunks - 1
        e = jnp.where(turn == 0, 0, jnp.where(turn == 1, last, turn - 1))
        velocity_chunk(0, e)

        @pl.when(turn == 0)
        def _():
            send_down(1, vel_dz)

        @pl.when(turn == min(1, last))
        def _():
            send_up(1, vel_dz)

        @pl.when((turn != 1) | (last == 1))
        def _():
            start_az(1, e)

        @pl.when((turn == last) & (last > 1))
        def _():
            start_az(1, last)

    each_chunk(first_velocity)
    for e in range(chunks):
        start_az(2, e)
    finish_az(0)
    finish_halos(0)

    receive_halos(1, vel_dz)

    def first_stress(e):
        stress_chunk(0, e)
        start_az(3, e)

        @pl.when(e == 0)
        def _():
            send_down(2, stress_dz)

        @pl.when(e == chunks - 1)
        def _():
            send_up(2, stress_dz)
            receive_far_top(1, far_v)

        @pl.when(e == 1)
        def _():
            receive_far_bottom(1, far_v)

        @pl.when(e > 0)
        def _():
            far_partials(1, far_v, e)
            far_stress_chunk(e - 1)

    each_chunk(first_stress)
    far_stress_chunk(chunks - 1)
    finish_az(1)
    finish_halos(1)

    receive_halos(2, stress_dz)
    to_out(s_az.at[:, inner], sa_out)
    to_out(s_rest.at[:, inner], sr_out)
    to_out(coef, coef_out)
    to_out(inv_r, inv_r_out)

    def second_velocity(e):
        velocity_chunk(1, e)
        start_az(4, e)

        @pl.when(e == 0)
        def _():
            send_down(3, vel_dz)

    each_chunk(second_velocity)
    send_up(3, vel_dz)
    to_out(v_az.at[:, inner], va_out.at[:, inner])
    to_out(v_rest.at[:, inner], vr_out.at[:, inner])
    to_out(mem, mem_out)
    receive_far_top(2, far_s)
    receive_far_bottom(2, far_s)
    for e in range(1, chunks):
        far_partials(2, far_s, e)
    each_chunk(far_velocity_chunk)
    to_out(far_v.at[:, pl.ds(2, 2), inner], fv_out)
    receive_halos(3, vel_dz)
    edge = pl.ds(depth, 1)
    to_out(v_az.at[pl.ds(0, 3), edge], va_out.at[pl.ds(0, 3), edge])
    to_out(v_rest.at[pl.ds(1, 1), edge], vr_out.at[pl.ds(1, 1), edge])
    to_out(partial, partial_out)
    finish_az(2)
    finish_az(3)
    finish_halos(2)
    for e in range(chunks):
        receive_az(4, e)
    finish_az(4)
    finish_halos(3)
    for copy in stores:
        copy.wait()


FAR_DZ = {1: (1, 2), 2: (2,)}


def finish_kernel(
    az_devices,
    source, radial_in, azim_in, coef_in, inv_r_in, partial_in, sa_in, sr_in, va_in, vr_in, fv_in,
    fn_in, mem_in,
    vel_out, str_out, mem_out,
    radial_k, azim_k, coef, inv_r, partial, s_az, s_rest, v_az, v_rest, far_v, far_new,
    rad_d, az_d,
    load_sem, load_chunk_sem, move_sem, chunk_sem,
):
    me_d = lax.axis_index("depth")
    depth, azims, radii = s_az.shape[1:]
    chunks = depth // 4
    others = range(az_devices - 1)
    gll_nodes, weights, derivative = gll_basis()
    stencil = weights[:, None] * derivative * 2.0

    def reader(ref, k):
        return lambda z: ref[k, z]

    def dz_at(read, below, base, j):
        if j == 0:
            total = weighted([(stencil[0, l], read(base + l)) for l in range(1, 5)])
            return (total + below) * np.float32(1.0 / (2.0 * weights[0]))
        return weighted([(2.0 * derivative[j, l], read(base + l)) for l in range(5)])

    def high_low(value, axis):
        high = value.astype(BF16)
        low = (value - high.astype(F32)).astype(BF16)
        return jnp.concatenate([high, low, high], axis=axis)

    def radial_part(blocks):
        rows = jnp.concatenate([block.reshape(4 * azims, radii) for block in blocks], axis=0)
        result = jnp.dot(high_low(rows, 1), radial_k[...], preferred_element_type=F32)
        rad_d[0 : len(blocks)] = result.reshape(len(blocks), 4, azims, radii)

    def azimuth_part(near, far, base):
        rows = azims
        for j in range(4):
            blocks = [jnp.concatenate([ref[f, base + j] for ref, f in near], axis=1)]
            for k in others:
                blocks.append(jnp.concatenate([ref[k, f, base + j] for ref, f in far], axis=1))
            column = jnp.concatenate(blocks, axis=0)
            result = jnp.dot(
                azim_k[0:rows, :], high_low(column, 0), preferred_element_type=F32
            )
            az_d[j] = result[0:azims]

    def az_at(j, f):
        return az_d[j, :, f * radii : (f + 1) * radii]

    def row_of(e):
        def row(index):
            return coef[index, pl.ds(e, 1), :]

        return row

    def shot_at(step, z):
        gain = np.float32(DT * SOURCE_GAIN * math.cos(0.9 * step))
        lane = lax.broadcasted_iota(jnp.int32, (1, radii), 1)
        wanted = jnp.zeros((1, radii), jnp.int32) + source[0]
        return jnp.where((wanted == me_d * depth + z) & (lane < 4 * RB), gain, np.float32(0.0))

    def stress_chunk(step, e):
        base = pl.multiple_of(4 * e, 4)
        planes = pl.ds(base, 4)
        radial_part([v_az[0, planes], v_az[2, planes], v_az[1, planes], v_rest[0, planes]])
        far = [(far_new, 0), (far_new, 1), (far_v, 0), (far_v, 1)]
        azimuth_part([(v_az, f) for f in range(4)], far, base)
        row = row_of(e)
        q = inv_r[...]
        for j in range(4):
            z = base + j
            vr, vt, wr = v_az[0, z], v_az[2, z], v_rest[0, z]
            dz = [
                dz_at(reader(ref, k), partial[f, e], base, j)
                for f, (ref, k) in enumerate(vel_dz)
            ]
            e_rr = rad_d[0, j]
            e_tt = q * (vr + az_at(j, 2))
            e_zz = dz[1]
            g_rt = q * (az_at(j, 0) - vt) + rad_d[1, j]
            g_rz = dz[0] + rad_d[2, j]
            g_tz = dz[2] + q * az_at(j, 1)
            div_v = e_rr + e_tt + e_zz
            div_w = rad_d[3, j] + q * (wr + az_at(j, 3)) + dz[3]
            bulk = row(LF) * div_v + row(BM) * div_w
            twice = 2.0 * row(MU)
            s_rest[0, z] = s_rest[0, z] + (bulk + twice * e_rr)
            s_az[1, z] = s_az[1, z] + (bulk + twice * e_tt)
            s_rest[1, z] = s_rest[1, z] + (bulk + twice * e_zz)
            s_az[0, z] = s_az[0, z] + row(MU) * g_rt
            s_rest[2, z] = s_rest[2, z] + row(MU) * g_rz
            s_az[2, z] = s_az[2, z] + row(MU) * g_tz
            s_az[3, z] = s_az[3, z] - (row(BM) * div_v + row(PM) * div_w) + shot_at(step, z)

    vel_dz = [(v_az, 0), (v_az, 1), (v_az, 2), (v_rest, 1)]

    def chunk_loads(e):
        planes = pl.ds(pl.multiple_of(4 * e, 4), 4)
        pairs = [(ref_in.at[:, planes], ref.at[:, planes]) for ref_in, ref in ((sa_in, s_az), (sr_in, s_rest))]
        pairs += [
            (ref_in.at[:, :, planes], ref.at[:, :, planes])
            for ref_in, ref in ((fv_in, far_v), (fn_in, far_new))
        ]
        return [
            pltpu.make_async_copy(src, dst, load_chunk_sem.at[e, i])
            for i, (src, dst) in enumerate(pairs)
        ]

    pairs = [(va_in, v_az), (vr_in, v_rest), (partial_in, partial), (radial_in, radial_k)]
    pairs += [(azim_in, azim_k), (coef_in, coef), (inv_r_in, inv_r)]
    loads = [pltpu.make_async_copy(src, dst, load_sem.at[i]) for i, (src, dst) in enumerate(pairs)]
    for copy in loads:
        copy.start()
    for e in range(chunks):
        for copy in chunk_loads(e):
            copy.start()
    for copy in loads:
        copy.wait()
    vel_place = [(v_az, 0), (v_az, 2), (v_az, 1), (v_rest, 0), (v_az, 3), (v_rest, 1)]
    stress_place = [(s_rest, 0), (s_az, 1), (s_rest, 1), (s_az, 0), (s_rest, 2), (s_az, 2), (s_az, 3)]
    moves = [(mem_in, mem_out)]
    moves += [(ref.at[k, pl.ds(0, depth)], vel_out.at[i]) for i, (ref, k) in enumerate(vel_place)]
    moves = [pltpu.make_async_copy(src, dst, move_sem.at[i]) for i, (src, dst) in enumerate(moves)]

    def chunk_stores(e):
        planes = pl.ds(pl.multiple_of(4 * e, 4), 4)
        return [
            pltpu.make_async_copy(ref.at[k, planes], str_out.at[i, planes], chunk_sem.at[e, i])
            for i, (ref, k) in enumerate(stress_place)
        ]

    def body(e, carry):
        for copy in chunk_loads(e):
            copy.wait()

        @pl.when(e == 0)
        def _():
            for copy in moves:
                copy.start()

        stress_chunk(STEPS - 1, e)
        for copy in chunk_stores(e):
            copy.start()
        return carry

    lax.fori_loop(0, chunks, body, 0)
    for copy in moves:
        copy.wait()
    for e in range(chunks):
        for copy in chunk_stores(e):
            copy.wait()


def on_device(depth_devices, az_devices, velocity, stress, memory, layer_ids, materials, jkd, source_depth):
    depth, azims, radii = velocity.shape[1:]
    chunks = depth // 4
    halves = 2 * STEPS
    others = max(az_devices - 1, 1)
    azim_total = azims * az_devices
    radial_high, radial_low = split_high_low(radial_operator(radii).T)
    radial_k = np.concatenate([radial_high, radial_high, radial_low], axis=0)
    azim_high, azim_low = split_high_low(azimuth_operator(azim_total))
    azim_k = np.concatenate([azim_high, azim_high, azim_low], axis=1)
    plane = (azims, radii)
    smem = pl.BlockSpec(memory_space=pltpu.SMEM)
    hbm = pl.BlockSpec(memory_space=pltpu.HBM)
    dma = pltpu.SemaphoreType.DMA
    constants = [radial_k, azim_k]
    small = [materials, jkd, layer_ids] + [jnp.asarray(value) for value in constants]

    def held(*shape):
        return pltpu.VMEM(shape + plane, F32)

    def whole(*shape):
        return jax.ShapeDtypeStruct(shape + plane, F32)

    coef_shape = (NCOEF, chunks, radii)
    parts = pl.pallas_call(
        functools.partial(step_kernel, depth_devices, az_devices),
        out_shape=(
            jax.ShapeDtypeStruct(coef_shape, F32),
            jax.ShapeDtypeStruct((1, radii), F32),
            whole(4, chunks),
            whole(4, depth),
            whole(3, depth),
            whole(4, depth + 1),
            whole(2, depth + 1),
            whole(others, 2, depth),
            whole(others, 2, depth),
            whole(12, depth),
        ),
        in_specs=[smem] + [hbm] * 8,
        out_specs=(hbm,) * 10,
        scratch_shapes=[pltpu.VMEM(value.shape, value.dtype) for value in small] + [
            held(12, depth),
            pltpu.VMEM((1, radii), F32),
            held(4, depth + 1),
            held(3, depth + 1),
            held(4, depth + 1),
            held(2, depth + 1),
            held(others, 4, depth + 1),
            held(others, 4, depth + 1),
            held(others, 1, depth),
            held(others, 1, depth),
            held(others, 3, depth),
            held(1, depth),
            held(1, depth),
            held(halves, 4),
            held(halves, 4),
            held(2, others, 2),
            held(2, others, 2),
            held(halves, 4),
            held(halves, 4),
            held(4, chunks),
            held(others, 2, chunks),
            pltpu.VMEM(coef_shape, F32),
            held(4, 4),
            pltpu.VMEM((4, azims, 4 * radii), F32),
            dma((19,)),
            dma((chunks, 4)),
            dma((11,)),
            dma((5, others, chunks)),
            dma((5, others, chunks)),
            dma((halves, others + 1)),
            dma((halves, others + 1)),
            dma((halves, others + 1)),
            dma((halves, others + 1)),
        ],
        compiler_params=pltpu.CompilerParams(
            collective_id=0, has_side_effects=True, vmem_limit_bytes=64 * 1024 * 1024
        ),
        cost_estimate=pl.CostEstimate(
            flops=10**9, bytes_accessed=2 * 25 * velocity.size // 6 * 4, transcendentals=0
        ),
        name="biot_steps",
    )(source_depth, *small, velocity, stress, memory)
    return tuple(pl.pallas_call(
        functools.partial(finish_kernel, az_devices),
        out_shape=tuple(jax.ShapeDtypeStruct(x.shape, x.dtype) for x in (velocity, stress, memory)),
        in_specs=[smem] + [hbm] * 12,
        out_specs=(hbm,) * 3,
        scratch_shapes=[
            pltpu.VMEM(radial_k.shape, BF16),
            pltpu.VMEM(azim_k.shape, BF16),
            pltpu.VMEM(coef_shape, F32),
            pltpu.VMEM((1, radii), F32),
            held(4, chunks),
            held(4, depth),
            held(3, depth),
            held(4, depth + 1),
            held(2, depth + 1),
            held(others, 2, depth),
            held(others, 2, depth),
            held(4, 4),
            pltpu.VMEM((4, azims, 4 * radii), F32),
            dma((7,)),
            dma((chunks, 4)),
            dma((7,)),
            dma((chunks, 7)),
        ],
        compiler_params=pltpu.CompilerParams(vmem_limit_bytes=64 * 1024 * 1024),
        cost_estimate=pl.CostEstimate(
            flops=10**9, bytes_accessed=2 * 25 * velocity.size // 6 * 4, transcendentals=0
        ),
        name="biot_finish",
    )(source_depth, *small[3:], *parts))


def solution(mesh):
    return jax.shard_map(
        functools.partial(on_device, mesh.shape["depth"], mesh.shape["az"]),
        mesh=mesh,
        in_specs=(
            P(None, "depth", "az", None),
            P(None, "depth", "az", None),
            P(None, "depth", "az", None),
            P("depth", None),
            P(),
            P(),
            P(),
        ),
        out_specs=(
            P(None, "depth", "az", None),
            P(None, "depth", "az", None),
            P(None, "depth", "az", None),
        ),
        check_vma=False,
    )
```

```python
import functools
import math

import jax
import jax.numpy as jnp
import numpy as np
from jax import lax
from jax.experimental import pallas as pl
from jax.experimental.pallas import tpu as pltpu
from jax.sharding import PartitionSpec as P

STEPS = 2
RB = 4


DT = 0.02
SOURCE_GAIN = 40.0
R_INNER = 1.0
MESH = pl.DeviceIdType.MESH
F32 = jnp.float32
BF16 = jnp.bfloat16


def gll_basis():
    root_value = math.sqrt(3.0 / 7.0)
    gll_nodes = np.array([-1.0, -root_value, 0.0, root_value, 1.0])
    weights = np.array([0.1, 49.0 / 90.0, 32.0 / 45.0, 49.0 / 90.0, 0.1])
    offsets = gll_nodes[:, None] - gll_nodes[None, :] + np.eye(5)
    factors = np.prod(offsets, axis=1)
    derivative = factors[:, None] / factors[None, :] / offsets
    diagonal_part = np.sum(1.0 / offsets, axis=1) - 1.0
    derivative = derivative * (1.0 - np.eye(5)) + np.eye(5) * diagonal_part[:, None]
    return (gll_nodes, weights, derivative)


def radial_operator(node_count):
    gll_nodes, weights, derivative = gll_basis()
    full_count = node_count + 1
    stencil = weights[:, None] * derivative * 2.0
    assembled = np.zeros((full_count, full_count))
    node_mass = np.zeros(full_count)
    for element in range(node_count // 4):
        assembled[4 * element : 4 * element + 5, 4 * element : 4 * element + 5] += stencil
        node_mass[4 * element : 4 * element + 5] += weights
    return (assembled / node_mass[:, None])[:node_count, :node_count]


def azimuth_operator(node_count):
    positions = np.arange(node_count)
    offsets = positions[:, None] - positions[None, :]
    wave_modes = np.arange(1, node_count // 2)
    phases = 2.0 * np.pi * offsets[:, :, None] * wave_modes[None, None, :] / node_count
    return -(2.0 / node_count) * np.sum(wave_modes * np.sin(phases), axis=2)


def split_high_low(matrix):
    matrix = np.asarray(matrix, np.float32)
    high = matrix.astype(jnp.bfloat16)
    low = (matrix - high.astype(np.float32)).astype(jnp.bfloat16)
    return high, low


A1, A2, A3, FA, OM, INV, LF, BM, MU, PM, NCOEF = 0, 1, 2, 3, 7, 8, 12, 13, 14, 15, 16


def weighted(terms):
    total = None
    for factor, value in terms:
        if abs(factor) < 1e-12:
            continue
        term = value * np.float32(factor)
        total = term if total is None else total + term
    return total


def step_kernel(
    depth_devices, az_devices,
    source, mats_in, jkd_in, ids_in, radial_in, azim_in, vel_in, str_in, mem_in,
    vel_out, str_out, mem_out,
    mats, jkd, ids, radial_k, azim_k,
    mem, inv_r, s_az, s_rest, v_az, v_rest, far_s, far_v, far_new, far_dw, far_psi, far_dt, dw, psi_t,
    halo_above, halo_below, far_above, far_below, up_stage, down_stage,
    partial, far_partial, coef, rad_d, az_d,
    load_sem, store_sem, chunk_sem, az_send, az_recv, up_send, up_recv, down_send, down_recv,
):
    me_d = lax.axis_index("depth")
    me_a = lax.axis_index("az")
    depth, azims, radii = mem.shape[1:]
    chunks = depth // 4
    others = range(az_devices - 1)
    has_up = me_d < depth_devices - 1
    has_down = me_d > 0
    gll_nodes, weights, derivative = gll_basis()
    stencil = weights[:, None] * derivative * 2.0

    inner = pl.ds(0, depth)
    stress_place = [(s_rest, 0), (s_az, 1), (s_rest, 1), (s_az, 0), (s_rest, 2), (s_az, 2), (s_az, 3)]
    vel_place = [(v_az, 0), (v_az, 2), (v_az, 1), (v_rest, 0), (v_az, 3), (v_rest, 1)]
    pairs = [(str_in.at[i], ref.at[k, inner]) for i, (ref, k) in enumerate(stress_place)]
    pairs += [(vel_in.at[i], ref.at[k, inner]) for i, (ref, k) in enumerate(vel_place)]
    pairs += [(mem_in, mem), (mats_in, mats), (jkd_in, jkd), (ids_in, ids)]
    pairs += [(radial_in, radial_k), (azim_in, azim_k)]
    loads = [
        pltpu.make_async_copy(src, dst, load_sem.at[i]) for i, (src, dst) in enumerate(pairs)
    ]
    for index in (1, 3, 5, 6, 14, 15, 16, 0, 2, 4, 17, 18, 7, 8, 9, 10, 11, 12, 13):
        loads[index].start()

    def other_az(k, sign):
        return lax.rem(me_a + (az_devices + sign * k), az_devices)

    barrier = pltpu.get_barrier_semaphore()

    def greet(where_d, where_a):
        pl.semaphore_signal(barrier, inc=1, device_id=(where_d, where_a), device_id_type=MESH)

    for k in range(1, az_devices):
        greet(me_d, other_az(k, 1))

    @pl.when(has_up)
    def _():
        for k in range(az_devices):
            greet(me_d + 1, other_az(k, 1))

    @pl.when(has_down)
    def _():
        for k in range(az_devices):
            greet(me_d - 1, other_az(k, 1))

    neighbours = has_up.astype(jnp.int32) + has_down.astype(jnp.int32)
    pl.semaphore_wait(barrier, (az_devices - 1) + az_devices * neighbours)

    exchanges = [
        (s_az, far_s, 4), (v_az, far_v, 4), (psi_t, far_psi, 1), (dw, far_dw, 1), (v_az, far_new, 2),
    ]

    def az_copies(which, e):
        source_ref, target_ref, count = exchanges[which]
        planes = pl.ds(pl.multiple_of(4 * e, 4), 4)
        return [
            pltpu.make_async_remote_copy(
                src_ref=source_ref.at[pl.ds(0, count), planes],
                dst_ref=target_ref.at[k, pl.ds(0, count), planes],
                send_sem=az_send.at[which, k, e],
                recv_sem=az_recv.at[which, k, e],
                device_id=(me_d, other_az(k + 1, -1)),
                device_id_type=MESH,
            )
            for k in others
        ]

    def start_az(which, e):
        for copy in az_copies(which, e):
            copy.start()

    def receive_az(which, e):
        for copy in az_copies(which, e):
            copy.wait_recv()

    far_fields = {1: (1, 2), 2: (1, 1)}

    def halo_copies(half, stage, near, far, send_sem, recv_sem, where_d):
        copies = [
            pltpu.make_async_remote_copy(
                src_ref=stage.at[half], dst_ref=near.at[half],
                send_sem=send_sem.at[half, 0], recv_sem=recv_sem.at[half, 0],
                device_id=(where_d, me_a), device_id_type=MESH,
            )
        ]
        if half in far_fields:
            first, count = far_fields[half]
            for k in others:
                copies.append(
                    pltpu.make_async_remote_copy(
                        src_ref=stage.at[half, pl.ds(first, count)],
                        dst_ref=far.at[half - 1, k, pl.ds(0, count)],
                        send_sem=send_sem.at[half, k + 1], recv_sem=recv_sem.at[half, k + 1],
                        device_id=(where_d, other_az(k + 1, -1)), device_id_type=MESH,
                    )
                )
        return copies

    def up_copies(half):
        return halo_copies(half, up_stage, halo_below, far_below, up_send, up_recv, me_d + 1)

    def down_copies(half):
        return halo_copies(half, down_stage, halo_above, far_above, down_send, down_recv, me_d - 1)

    stress_dz = [(s_rest, 2), (s_az, 2), (s_rest, 1), (s_az, 3)]
    vel_dz = [(v_az, 0), (v_az, 1), (v_az, 2), (v_rest, 1)]

    def top_of(read, base):
        return weighted([(stencil[4, l], read(base + l)) for l in range(4)])

    def bottom_of(read):
        return weighted([(stencil[0, l] * (2.0 if l == 0 else 1.0), read(l)) for l in range(5)])

    def reader(ref, k):
        return lambda z: ref[k, z]

    def far_reader(ref, k, f):
        return lambda z: ref[k, f, z]

    def send_down(half, dz_fields):
        for f, (ref, k) in enumerate(dz_fields):
            down_stage[half, f] = ref[k, 0]

        @pl.when(has_down)
        def _():
            for copy in down_copies(half):
                copy.start()

    def send_up(half, dz_fields):
        for f, (ref, k) in enumerate(dz_fields):
            up_stage[half, f] = top_of(reader(ref, k), depth - 4)

        @pl.when(has_up)
        def _():
            for copy in up_copies(half):
                copy.start()

    def receive_halos(half, dz_fields):
        for e in range(1, chunks):
            for f, (ref, k) in enumerate(dz_fields):
                partial[f, e] = top_of(reader(ref, k), 4 * (e - 1))

        @pl.when(has_up)
        def _():
            down_copies(half)[0].wait_recv()
            for f, (ref, k) in enumerate(dz_fields):
                ref[k, depth] = halo_above[half, f]

        @pl.when(jnp.logical_not(has_up))
        def _():
            for f, (ref, k) in enumerate(dz_fields):
                ref[k, depth] = jnp.zeros((azims, radii), F32)

        @pl.when(has_down)
        def _():
            up_copies(half)[0].wait_recv()
            partial[:, 0] = halo_below[half]

        @pl.when(jnp.logical_not(has_down))
        def _():
            for f, (ref, k) in enumerate(dz_fields):
                partial[f, 0] = bottom_of(reader(ref, k))

    def far_list(half):
        return [(k, i, f) for k in others for i, f in enumerate(FAR_DZ[half])]

    def far_partials(half, ref, e):
        for k, i, f in far_list(half):
            far_partial[k, i, e] = top_of(far_reader(ref, k, f), 4 * (e - 1))

    def receive_far_top(half, ref):
        @pl.when(has_up)
        def _():
            for copy in down_copies(half)[1:]:
                copy.wait_recv()
            for k, i, f in far_list(half):
                ref[k, f, depth] = far_above[half - 1, k, i]

        @pl.when(jnp.logical_not(has_up))
        def _():
            for k, i, f in far_list(half):
                ref[k, f, depth] = jnp.zeros((azims, radii), F32)

    def receive_far_bottom(half, ref):
        @pl.when(has_down)
        def _():
            for copy in up_copies(half)[1:]:
                copy.wait_recv()
            for k, i, f in far_list(half):
                far_partial[k, i, 0] = far_below[half - 1, k, i]

        @pl.when(jnp.logical_not(has_down))
        def _():
            for k, i, f in far_list(half):
                far_partial[k, i, 0] = bottom_of(far_reader(ref, k, f))

    def finish_az(which):
        for e in range(chunks):
            for copy in az_copies(which, e):
                copy.wait_send()

    def finish_halos(half):
        @pl.when(has_up)
        def _():
            for copy in up_copies(half):
                copy.wait_send()

        @pl.when(has_down)
        def _():
            for copy in down_copies(half):
                copy.wait_send()

    def dz_at(read, below, base, j):
        if j == 0:
            total = weighted([(stencil[0, l], read(base + l)) for l in range(1, 5)])
            return (total + below) * np.float32(1.0 / (2.0 * weights[0]))
        return weighted([(2.0 * derivative[j, l], read(base + l)) for l in range(5)])

    def high_low(value, axis):
        high = value.astype(BF16)
        low = (value - high.astype(F32)).astype(BF16)
        return jnp.concatenate([high, low, high], axis=axis)

    def radial_part(blocks):
        rows = jnp.concatenate([block.reshape(4 * azims, radii) for block in blocks], axis=0)
        result = jnp.dot(high_low(rows, 1), radial_k[...], preferred_element_type=F32)
        rad_d[0 : len(blocks)] = result.reshape(len(blocks), 4, azims, radii)

    def azimuth_part(near, far, base, kept):
        rows = azims * az_devices if kept else azims
        for j in range(4):
            blocks = [jnp.concatenate([ref[f, base + j] for ref, f in near], axis=1)]
            for k in others:
                blocks.append(jnp.concatenate([ref[k, f, base + j] for ref, f in far], axis=1))
            column = jnp.concatenate(blocks, axis=0)
            result = jnp.dot(
                azim_k[0:rows, :], high_low(column, 0), preferred_element_type=F32
            )
            az_d[j] = result[0:azims]
            for i, f in enumerate(kept):
                for k in others:
                    far_dt[k, i, base + j] = result[
                        (k + 1) * azims : (k + 2) * azims, f * radii : (f + 1) * radii
                    ]

    def az_at(j, f):
        return az_d[j, :, f * radii : (f + 1) * radii]

    def row_of(e):
        def row(index):
            return coef[index, pl.ds(e, 1), :]

        return row

    def shot_at(step, z):
        gain = np.float32(DT * SOURCE_GAIN * math.cos(0.9 * step))
        lane = lax.broadcasted_iota(jnp.int32, (1, radii), 1)
        wanted = jnp.zeros((1, radii), jnp.int32) + source[0]
        return jnp.where((wanted == me_d * depth + z) & (lane < 4 * RB), gain, np.float32(0.0))

    def velocity_chunk(step, e):
        base = pl.multiple_of(4 * e, 4)
        planes = pl.ds(base, 4)
        row = row_of(e)
        if step == 0:
            receive_az(0, e)
        else:
            receive_az(3, e)
            for k in others:
                for j in range(4):
                    z = base + j
                    far_s[k, 1, z] = far_s[k, 1, z] + row(BM) * far_dw[k, 0, z]
                    far_s[k, 3, z] = far_s[k, 3, z] - row(PM) * far_dw[k, 0, z]
        radial_part([s_rest[0, planes], s_az[0, planes], s_rest[2, planes], s_az[3, planes]])
        azimuth_part(
            [(s_az, f) for f in range(4)], [(far_s, f) for f in range(4)], base,
            (1, 3) if step == 1 else (),
        )
        q = inv_r[...]
        for j in range(4):
            z = base + j
            rt, tt = s_az[0, z], s_az[1, z]
            rr, rz = s_rest[0, z], s_rest[2, z]
            dz = [
                dz_at(reader(ref, k), partial[f, e], base, j)
                for f, (ref, k) in enumerate(stress_dz)
            ]
            div = [
                rad_d[0, j] + q * (az_at(j, 0) + (rr - tt)) + dz[0],
                rad_d[1, j] + q * (az_at(j, 1) + 2.0 * rt) + dz[1],
                rad_d[2, j] + q * (az_at(j, 2) + rz) + dz[2],
            ]
            grad = [rad_d[3, j], q * az_at(j, 3), dz[3]]
            solid = [(v_az, 0), (v_az, 2), (v_az, 1)]
            fluid = [(v_rest, 0), (v_az, 3), (v_rest, 1)]
            for c in range(3):
                psi = [mem[3 * pole + c, z] for pole in range(4)]
                resist = grad[c]
                for pole in range(4):
                    resist = resist + row(FA + pole) * psi[pole]
                ref, k = solid[c]
                ref[k, z] = ref[k, z] + (row(A1) * div[c] + row(A2) * resist)
                change = -(row(A2) * div[c] + row(A3) * resist)
                ref, k = fluid[c]
                fresh = ref[k, z] + change
                ref[k, z] = fresh
                change = change + row(OM) * fresh
                psi = [(psi[pole] + change) * row(INV + pole) for pole in range(4)]
                for pole in range(4):
                    mem[3 * pole + c, z] = psi[pole]
                if c == 1 and step == 0:
                    total = row(FA) * psi[0]
                    for pole in range(1, 4):
                        total = total + row(FA + pole) * psi[pole]
                    psi_t[0, z] = total

    def stress_chunk(step, e):
        base = pl.multiple_of(4 * e, 4)
        planes = pl.ds(base, 4)
        radial_part([v_az[0, planes], v_az[2, planes], v_az[1, planes], v_rest[0, planes]])
        if step == 0:
            receive_az(1, e)
            far = [(far_v, f) for f in range(4)]
        else:
            receive_az(4, e)
            far = [(far_new, 0), (far_new, 1), (far_v, 2), (far_v, 3)]
        azimuth_part([(v_az, f) for f in range(4)], far, base, (0, 1, 2) if step == 0 else ())
        row = row_of(e)
        q = inv_r[...]
        for j in range(4):
            z = base + j
            vr, vt, wr = v_az[0, z], v_az[2, z], v_rest[0, z]
            dz = [
                dz_at(reader(ref, k), partial[f, e], base, j)
                for f, (ref, k) in enumerate(vel_dz)
            ]
            e_rr = rad_d[0, j]
            e_tt = q * (vr + az_at(j, 2))
            e_zz = dz[1]
            g_rt = q * (az_at(j, 0) - vt) + rad_d[1, j]
            g_rz = dz[0] + rad_d[2, j]
            g_tz = dz[2] + q * az_at(j, 1)
            div_v = e_rr + e_tt + e_zz
            div_w = rad_d[3, j] + q * (wr + az_at(j, 3)) + dz[3]
            if step == 0:
                dw[0, z] = div_w
            bulk = row(LF) * div_v + row(BM) * div_w
            twice = 2.0 * row(MU)
            s_rest[0, z] = s_rest[0, z] + (bulk + twice * e_rr)
            s_az[1, z] = s_az[1, z] + (bulk + twice * e_tt)
            s_rest[1, z] = s_rest[1, z] + (bulk + twice * e_zz)
            s_az[0, z] = s_az[0, z] + row(MU) * g_rt
            s_rest[2, z] = s_rest[2, z] + row(MU) * g_rz
            s_az[2, z] = s_az[2, z] + row(MU) * g_tz
            s_az[3, z] = s_az[3, z] - (row(BM) * div_v + row(PM) * div_w) + shot_at(step, z)

    def far_stress_chunk(e):
        base = pl.multiple_of(4 * e, 4)
        planes = pl.ds(base, 4)
        row = row_of(e)
        q = inv_r[...]
        for k in others:
            radial_part([far_v[k, 0, planes], far_v[k, 2, planes]])
            for j in range(4):
                z = base + j
                vr, vt = far_v[k, 0, z], far_v[k, 2, z]
                dz_vz = dz_at(far_reader(far_v, k, 1), far_partial[k, 0, e], base, j)
                dz_vt = dz_at(far_reader(far_v, k, 2), far_partial[k, 1, e], base, j)
                e_tt = q * (vr + far_dt[k, 2, z])
                div_v = rad_d[0, j] + e_tt + dz_vz
                g_rt = q * (far_dt[k, 0, z] - vt) + rad_d[1, j]
                g_tz = dz_vt + q * far_dt[k, 1, z]
                far_s[k, 0, z] = far_s[k, 0, z] + row(MU) * g_rt
                far_s[k, 1, z] = far_s[k, 1, z] + (row(LF) * div_v + 2.0 * row(MU) * e_tt)
                far_s[k, 2, z] = far_s[k, 2, z] + row(MU) * g_tz
                far_s[k, 3, z] = far_s[k, 3, z] - row(BM) * div_v + shot_at(0, z)

    def far_velocity_chunk(e):
        base = pl.multiple_of(4 * e, 4)
        planes = pl.ds(base, 4)
        row = row_of(e)
        q = inv_r[...]
        receive_az(2, e)
        for k in others:
            radial_part([far_s[k, 0, planes]])
            for j in range(4):
                z = base + j
                dz_tz = dz_at(far_reader(far_s, k, 2), far_partial[k, 0, e], base, j)
                div = rad_d[0, j] + q * (far_dt[k, 0, z] + 2.0 * far_s[k, 0, z]) + dz_tz
                resist = q * far_dt[k, 1, z] + far_psi[k, 0, z]
                far_v[k, 2, z] = far_v[k, 2, z] + (row(A1) * div + row(A2) * resist)
                far_v[k, 3, z] = far_v[k, 3, z] - (row(A2) * div + row(A3) * resist)

    def each_chunk(body):
        def wrapped(e, carry):
            body(e)
            return carry

        lax.fori_loop(0, chunks, wrapped, 0)

    for index in (1, 3, 5, 6):
        loads[index].wait()
    order = [0] + ([chunks - 1] if chunks > 1 else []) + list(range(1, chunks - 1))
    for e in order:
        start_az(0, e)
    for index in (0, 2, 4):
        loads[index].wait()
    send_down(0, stress_dz)
    send_up(0, stress_dz)
    for index in range(14, 19):
        loads[index].wait()

    elements = ids.shape[1]
    spread = lax.broadcasted_iota(jnp.int32, (elements, radii), 0) == (
        lax.broadcasted_iota(jnp.int32, (elements, radii), 1) >> 2
    )
    ids_node = jnp.dot(
        ids[...].astype(F32).astype(BF16), spread.astype(F32).astype(BF16),
        preferred_element_type=F32,
    )
    node = lax.broadcasted_iota(jnp.int32, (1, radii), 1)
    place = node & 3
    inside = jnp.zeros((1, radii), F32)
    for j in range(1, 4):
        inside = jnp.where(place == j, np.float32(0.5 * (1.0 + gll_nodes[j])), inside)
    inv_r[...] = 1.0 / (np.float32(R_INNER) + (node >> 2).astype(F32) + inside)

    def pick(table, column):
        value = jnp.zeros_like(ids_node)
        for r in range(8):
            value = jnp.where(ids_node == float(r), table[r : r + 1, column : column + 1], value)
        return value

    lame_zero, shear, modulus, coupling, rho, rho_f, tort, fric = [pick(mats, c) for c in range(8)]
    omega = pick(jkd, 0)
    rho_w = rho_f * tort
    scale = DT / (rho * rho_w - rho_f * rho_f)
    coef[A1] = rho_w * scale
    coef[A2] = rho_f * scale
    coef[A3] = rho * scale
    for pole in range(4):
        coef[FA + pole] = fric * pick(jkd, 1 + pole)
        coef[INV + pole] = 1.0 / (1.0 + DT * (pick(jkd, 5 + pole) + omega))
    coef[OM] = DT * omega
    coef[LF] = DT * (lame_zero + coupling * coupling * modulus)
    coef[BM] = DT * coupling * modulus
    coef[MU] = DT * shear
    coef[PM] = DT * modulus

    for index in range(7, 14):
        loads[index].wait()

    stores = []

    def to_out(src, dst):
        copy = pltpu.make_async_copy(src, dst, store_sem.at[len(stores)])
        copy.start()
        stores.append(copy)

    receive_halos(0, stress_dz)

    def first_velocity(turn):
        last = chunks - 1
        e = jnp.where(turn == 0, 0, jnp.where(turn == 1, last, turn - 1))
        velocity_chunk(0, e)

        @pl.when(turn == 0)
        def _():
            send_down(1, vel_dz)

        @pl.when(turn == min(1, last))
        def _():
            send_up(1, vel_dz)

        @pl.when((turn != 1) | (last == 1))
        def _():
            start_az(1, e)

        @pl.when((turn == last) & (last > 1))
        def _():
            start_az(1, last)

    each_chunk(first_velocity)
    for e in range(chunks):
        start_az(2, e)
    finish_az(0)
    finish_halos(0)

    receive_halos(1, vel_dz)

    def first_stress(e):
        stress_chunk(0, e)
        start_az(3, e)

        @pl.when(e == 0)
        def _():
            send_down(2, stress_dz)

        @pl.when(e == chunks - 1)
        def _():
            send_up(2, stress_dz)
            receive_far_top(1, far_v)

        @pl.when(e == 1)
        def _():
            receive_far_bottom(1, far_v)

        @pl.when(e > 0)
        def _():
            far_partials(1, far_v, e)
            far_stress_chunk(e - 1)

    each_chunk(first_stress)
    far_stress_chunk(chunks - 1)
    finish_az(1)
    finish_halos(1)

    receive_halos(2, stress_dz)

    def second_velocity(e):
        velocity_chunk(1, e)
        start_az(4, e)

        @pl.when(e == 0)
        def _():
            send_down(3, vel_dz)

    each_chunk(second_velocity)
    send_up(3, vel_dz)
    for i, (ref, k) in enumerate(vel_place):
        to_out(ref.at[k, inner], vel_out.at[i])
    to_out(mem, mem_out)
    receive_far_top(2, far_s)
    receive_far_bottom(2, far_s)
    for e in range(1, chunks):
        far_partials(2, far_s, e)
    each_chunk(far_velocity_chunk)
    finish_az(2)
    finish_az(3)
    finish_halos(2)

    receive_halos(3, vel_dz)

    def chunk_stores(e):
        planes = pl.ds(pl.multiple_of(4 * e, 4), 4)
        return [
            pltpu.make_async_copy(ref.at[k, planes], str_out.at[i, planes], chunk_sem.at[e, i])
            for i, (ref, k) in enumerate(stress_place)
        ]

    def second_stress(e):
        stress_chunk(1, e)
        for copy in chunk_stores(e):
            copy.start()

    each_chunk(second_stress)
    finish_az(4)
    finish_halos(3)
    for copy in stores:
        copy.wait()
    for e in range(chunks):
        for copy in chunk_stores(e):
            copy.wait()


FAR_DZ = {1: (1, 2), 2: (2,)}


def deliver_kernel(vel_in, str_in, mem_in, vel_out, str_out, mem_out, held, load_sem, store_sem):
    rows = [(src.at[i], dst.at[i]) for src, dst in ((mem_in, mem_out), (str_in, str_out), (vel_in, vel_out))
            for i in range(src.shape[0])]
    loads = [
        pltpu.make_async_copy(src, held.at[i], load_sem.at[i]) for i, (src, dst) in enumerate(rows)
    ]
    stores = [
        pltpu.make_async_copy(held.at[i], dst, store_sem.at[i]) for i, (src, dst) in enumerate(rows)
    ]
    for copy in loads:
        copy.start()
    for load, store in zip(loads, stores):
        load.wait()
        store.start()
    for copy in stores:
        copy.wait()


def on_device(depth_devices, az_devices, velocity, stress, memory, layer_ids, materials, jkd, source_depth):
    depth, azims, radii = velocity.shape[1:]
    chunks = depth // 4
    halves = 2 * STEPS
    others = max(az_devices - 1, 1)
    azim_total = azims * az_devices
    radial_high, radial_low = split_high_low(radial_operator(radii).T)
    radial_k = np.concatenate([radial_high, radial_high, radial_low], axis=0)
    azim_high, azim_low = split_high_low(azimuth_operator(azim_total))
    azim_k = np.concatenate([azim_high, azim_high, azim_low], axis=1)
    plane = (azims, radii)
    smem = pl.BlockSpec(memory_space=pltpu.SMEM)
    hbm = pl.BlockSpec(memory_space=pltpu.HBM)
    dma = pltpu.SemaphoreType.DMA
    constants = [radial_k, azim_k]
    small = [materials, jkd, layer_ids] + [jnp.asarray(value) for value in constants]

    def held(*shape):
        return pltpu.VMEM(shape + plane, F32)

    results = pl.pallas_call(
        functools.partial(step_kernel, depth_devices, az_devices),
        out_shape=tuple(jax.ShapeDtypeStruct(x.shape, x.dtype) for x in (velocity, stress, memory)),
        in_specs=[smem] + [hbm] * 8,
        out_specs=(hbm, hbm, hbm),
        scratch_shapes=[pltpu.VMEM(value.shape, value.dtype) for value in small] + [
            held(12, depth),
            pltpu.VMEM((1, radii), F32),
            held(4, depth + 1),
            held(3, depth + 1),
            held(4, depth + 1),
            held(2, depth + 1),
            held(others, 4, depth + 1),
            held(others, 4, depth + 1),
            held(others, 2, depth),
            held(others, 1, depth),
            held(others, 1, depth),
            held(others, 3, depth),
            held(1, depth),
            held(1, depth),
            held(halves, 4),
            held(halves, 4),
            held(2, others, 2),
            held(2, others, 2),
            held(halves, 4),
            held(halves, 4),
            held(4, chunks),
            held(others, 2, chunks),
            pltpu.VMEM((NCOEF, chunks, radii), F32),
            held(4, 4),
            pltpu.VMEM((4, azims, 4 * radii), F32),
            dma((19,)),
            dma((7,)),
            dma((chunks, 7)),
            dma((5, others, chunks)),
            dma((5, others, chunks)),
            dma((halves, others + 1)),
            dma((halves, others + 1)),
            dma((halves, others + 1)),
            dma((halves, others + 1)),
        ],
        compiler_params=pltpu.CompilerParams(
            collective_id=0, has_side_effects=True, vmem_limit_bytes=64 * 1024 * 1024
        ),
        cost_estimate=pl.CostEstimate(
            flops=10**9, bytes_accessed=2 * 25 * velocity.size // 6 * 4, transcendentals=0
        ),
        name="biot_steps",
    )(source_depth, *small, velocity, stress, memory)
    return tuple(pl.pallas_call(
        deliver_kernel,
        out_shape=tuple(jax.ShapeDtypeStruct(x.shape, x.dtype) for x in results),
        in_specs=[hbm] * 3,
        out_specs=(hbm,) * 3,
        scratch_shapes=[held(25, depth), dma((25,)), dma((25,))],
        compiler_params=pltpu.CompilerParams(vmem_limit_bytes=64 * 1024 * 1024),
        cost_estimate=pl.CostEstimate(
            flops=0, bytes_accessed=2 * 25 * velocity.size // 6 * 4, transcendentals=0
        ),
        name="deliver",
    )(*results))


def solution(mesh):
    return jax.shard_map(
        functools.partial(on_device, mesh.shape["depth"], mesh.shape["az"]),
        mesh=mesh,
        in_specs=(
            P(None, "depth", "az", None),
            P(None, "depth", "az", None),
            P(None, "depth", "az", None),
            P("depth", None),
            P(),
            P(),
            P(),
        ),
        out_specs=(
            P(None, "depth", "az", None),
            P(None, "depth", "az", None),
            P(None, "depth", "az", None),
        ),
        check_vma=False,
    )
```

```python
import functools
import math

import jax
import jax.numpy as jnp
import numpy as np
from jax import lax
from jax.experimental import pallas as pl
from jax.experimental.pallas import tpu as pltpu
from jax.sharding import PartitionSpec as P

STEPS = 2
RB = 4


DT = 0.02
SOURCE_GAIN = 40.0
R_INNER = 1.0
MESH = pl.DeviceIdType.MESH
F32 = jnp.float32
BF16 = jnp.bfloat16


def gll_basis():
    root_value = math.sqrt(3.0 / 7.0)
    gll_nodes = np.array([-1.0, -root_value, 0.0, root_value, 1.0])
    weights = np.array([0.1, 49.0 / 90.0, 32.0 / 45.0, 49.0 / 90.0, 0.1])
    offsets = gll_nodes[:, None] - gll_nodes[None, :] + np.eye(5)
    factors = np.prod(offsets, axis=1)
    derivative = factors[:, None] / factors[None, :] / offsets
    diagonal_part = np.sum(1.0 / offsets, axis=1) - 1.0
    derivative = derivative * (1.0 - np.eye(5)) + np.eye(5) * diagonal_part[:, None]
    return (gll_nodes, weights, derivative)


def radial_operator(node_count):
    gll_nodes, weights, derivative = gll_basis()
    full_count = node_count + 1
    stencil = weights[:, None] * derivative * 2.0
    assembled = np.zeros((full_count, full_count))
    node_mass = np.zeros(full_count)
    for element in range(node_count // 4):
        assembled[4 * element : 4 * element + 5, 4 * element : 4 * element + 5] += stencil
        node_mass[4 * element : 4 * element + 5] += weights
    return (assembled / node_mass[:, None])[:node_count, :node_count]


def azimuth_operator(node_count):
    positions = np.arange(node_count)
    offsets = positions[:, None] - positions[None, :]
    wave_modes = np.arange(1, node_count // 2)
    phases = 2.0 * np.pi * offsets[:, :, None] * wave_modes[None, None, :] / node_count
    return -(2.0 / node_count) * np.sum(wave_modes * np.sin(phases), axis=2)


def split_high_low(matrix):
    matrix = np.asarray(matrix, np.float32)
    high = matrix.astype(jnp.bfloat16)
    low = (matrix - high.astype(np.float32)).astype(jnp.bfloat16)
    return high, low


A1, A2, A3, FA, OM, INV, LF, BM, MU, PM, NCOEF = 0, 1, 2, 3, 7, 8, 12, 13, 14, 15, 16


def weighted(terms):
    total = None
    for factor, value in terms:
        if abs(factor) < 1e-12:
            continue
        term = value * np.float32(factor)
        total = term if total is None else total + term
    return total


def step_kernel(
    depth_devices, az_devices,
    source, mats_in, jkd_in, ids_in, radial_in, azim_in, vel_in, str_in, mem_in,
    vel_out, str_out, mem_out,
    mats, jkd, ids, radial_k, azim_k,
    mem, inv_r, s_az, s_rest, v_az, v_rest, far_s, far_v, far_new, far_dw, far_psi, far_dt, dw, psi_t,
    halo_above, halo_below, far_above, far_below, up_stage, down_stage,
    partial, far_partial, coef, rad_d, az_d,
    load_sem, first_sem, store_sem, chunk_sem, az_send, az_recv, up_send, up_recv, down_send, down_recv,
):
    me_d = lax.axis_index("depth")
    me_a = lax.axis_index("az")
    depth, azims, radii = mem.shape[1:]
    chunks = depth // 4
    others = range(az_devices - 1)
    has_up = me_d < depth_devices - 1
    has_down = me_d > 0
    gll_nodes, weights, derivative = gll_basis()
    stencil = weights[:, None] * derivative * 2.0

    inner = pl.ds(0, depth)
    stress_place = [(s_rest, 0), (s_az, 1), (s_rest, 1), (s_az, 0), (s_rest, 2), (s_az, 2), (s_az, 3)]
    vel_place = [(v_az, 0), (v_az, 2), (v_az, 1), (v_rest, 0), (v_az, 3), (v_rest, 1)]
    pairs = [(str_in.at[i], ref.at[k, inner]) for i, (ref, k) in enumerate(stress_place)]
    pairs += [(vel_in.at[i], ref.at[k, inner]) for i, (ref, k) in enumerate(vel_place)]
    pairs += [(mem_in, mem), (mats_in, mats), (jkd_in, jkd), (ids_in, ids)]
    pairs += [(radial_in, radial_k), (azim_in, azim_k)]
    loads = [
        pltpu.make_async_copy(src, dst, load_sem.at[i]) for i, (src, dst) in enumerate(pairs)
    ]
    order = [0] + ([chunks - 1] if chunks > 1 else []) + list(range(1, chunks - 1))

    def first_loads(e):
        planes = pl.ds(4 * e, 4)
        return [
            pltpu.make_async_copy(str_in.at[i, planes], s_az.at[k, planes], first_sem.at[e, k])
            for k, i in enumerate((3, 1, 5, 6))
        ]

    for e in order:
        for copy in first_loads(e):
            copy.start()
    for index in (14, 15, 16, 0, 2, 4, 17, 18, 7, 8, 9, 10, 11, 12, 13):
        loads[index].start()

    def other_az(k, sign):
        return lax.rem(me_a + (az_devices + sign * k), az_devices)

    barrier = pltpu.get_barrier_semaphore()

    def greet(where_d, where_a):
        pl.semaphore_signal(barrier, inc=1, device_id=(where_d, where_a), device_id_type=MESH)

    for k in range(1, az_devices):
        greet(me_d, other_az(k, 1))

    @pl.when(has_up)
    def _():
        for k in range(az_devices):
            greet(me_d + 1, other_az(k, 1))

    @pl.when(has_down)
    def _():
        for k in range(az_devices):
            greet(me_d - 1, other_az(k, 1))

    neighbours = has_up.astype(jnp.int32) + has_down.astype(jnp.int32)
    pl.semaphore_wait(barrier, (az_devices - 1) + az_devices * neighbours)

    exchanges = [
        (s_az, far_s, 4), (v_az, far_v, 4), (psi_t, far_psi, 1), (dw, far_dw, 1), (v_az, far_new, 2),
    ]

    def az_copies(which, e):
        source_ref, target_ref, count = exchanges[which]
        planes = pl.ds(pl.multiple_of(4 * e, 4), 4)
        return [
            pltpu.make_async_remote_copy(
                src_ref=source_ref.at[pl.ds(0, count), planes],
                dst_ref=target_ref.at[k, pl.ds(0, count), planes],
                send_sem=az_send.at[which, k, e],
                recv_sem=az_recv.at[which, k, e],
                device_id=(me_d, other_az(k + 1, -1)),
                device_id_type=MESH,
            )
            for k in others
        ]

    def start_az(which, e):
        for copy in az_copies(which, e):
            copy.start()

    def receive_az(which, e):
        for copy in az_copies(which, e):
            copy.wait_recv()

    far_fields = {1: (1, 2), 2: (1, 1)}

    def halo_copies(half, stage, near, far, send_sem, recv_sem, where_d):
        copies = [
            pltpu.make_async_remote_copy(
                src_ref=stage.at[half], dst_ref=near.at[half],
                send_sem=send_sem.at[half, 0], recv_sem=recv_sem.at[half, 0],
                device_id=(where_d, me_a), device_id_type=MESH,
            )
        ]
        if half in far_fields:
            first, count = far_fields[half]
            for k in others:
                copies.append(
                    pltpu.make_async_remote_copy(
                        src_ref=stage.at[half, pl.ds(first, count)],
                        dst_ref=far.at[half - 1, k, pl.ds(0, count)],
                        send_sem=send_sem.at[half, k + 1], recv_sem=recv_sem.at[half, k + 1],
                        device_id=(where_d, other_az(k + 1, -1)), device_id_type=MESH,
                    )
                )
        return copies

    def up_copies(half):
        return halo_copies(half, up_stage, halo_below, far_below, up_send, up_recv, me_d + 1)

    def down_copies(half):
        return halo_copies(half, down_stage, halo_above, far_above, down_send, down_recv, me_d - 1)

    stress_dz = [(s_rest, 2), (s_az, 2), (s_rest, 1), (s_az, 3)]
    vel_dz = [(v_az, 0), (v_az, 1), (v_az, 2), (v_rest, 1)]

    def top_of(read, base):
        return weighted([(stencil[4, l], read(base + l)) for l in range(4)])

    def bottom_of(read):
        return weighted([(stencil[0, l] * (2.0 if l == 0 else 1.0), read(l)) for l in range(5)])

    def reader(ref, k):
        return lambda z: ref[k, z]

    def far_reader(ref, k, f):
        return lambda z: ref[k, f, z]

    def send_down(half, dz_fields):
        for f, (ref, k) in enumerate(dz_fields):
            down_stage[half, f] = ref[k, 0]

        @pl.when(has_down)
        def _():
            for copy in down_copies(half):
                copy.start()

    def send_up(half, dz_fields):
        for f, (ref, k) in enumerate(dz_fields):
            up_stage[half, f] = top_of(reader(ref, k), depth - 4)

        @pl.when(has_up)
        def _():
            for copy in up_copies(half):
                copy.start()

    def receive_halos(half, dz_fields):
        for e in range(1, chunks):
            for f, (ref, k) in enumerate(dz_fields):
                partial[f, e] = top_of(reader(ref, k), 4 * (e - 1))

        @pl.when(has_up)
        def _():
            down_copies(half)[0].wait_recv()
            for f, (ref, k) in enumerate(dz_fields):
                ref[k, depth] = halo_above[half, f]

        @pl.when(jnp.logical_not(has_up))
        def _():
            for f, (ref, k) in enumerate(dz_fields):
                ref[k, depth] = jnp.zeros((azims, radii), F32)

        @pl.when(has_down)
        def _():
            up_copies(half)[0].wait_recv()
            partial[:, 0] = halo_below[half]

        @pl.when(jnp.logical_not(has_down))
        def _():
            for f, (ref, k) in enumerate(dz_fields):
                partial[f, 0] = bottom_of(reader(ref, k))

    def far_list(half):
        return [(k, i, f) for k in others for i, f in enumerate(FAR_DZ[half])]

    def far_partials(half, ref, e):
        for k, i, f in far_list(half):
            far_partial[k, i, e] = top_of(far_reader(ref, k, f), 4 * (e - 1))

    def receive_far_top(half, ref):
        @pl.when(has_up)
        def _():
            for copy in down_copies(half)[1:]:
                copy.wait_recv()
            for k, i, f in far_list(half):
                ref[k, f, depth] = far_above[half - 1, k, i]

        @pl.when(jnp.logical_not(has_up))
        def _():
            for k, i, f in far_list(half):
                ref[k, f, depth] = jnp.zeros((azims, radii), F32)

    def receive_far_bottom(half, ref):
        @pl.when(has_down)
        def _():
            for copy in up_copies(half)[1:]:
                copy.wait_recv()
            for k, i, f in far_list(half):
                far_partial[k, i, 0] = far_below[half - 1, k, i]

        @pl.when(jnp.logical_not(has_down))
        def _():
            for k, i, f in far_list(half):
                far_partial[k, i, 0] = bottom_of(far_reader(ref, k, f))

    def finish_az(which):
        for e in range(chunks):
            for copy in az_copies(which, e):
                copy.wait_send()

    def finish_halos(half):
        @pl.when(has_up)
        def _():
            for copy in up_copies(half):
                copy.wait_send()

        @pl.when(has_down)
        def _():
            for copy in down_copies(half):
                copy.wait_send()

    def dz_at(read, below, base, j):
        if j == 0:
            total = weighted([(stencil[0, l], read(base + l)) for l in range(1, 5)])
            return (total + below) * np.float32(1.0 / (2.0 * weights[0]))
        return weighted([(2.0 * derivative[j, l], read(base + l)) for l in range(5)])

    def high_low(value, axis):
        high = value.astype(BF16)
        low = (value - high.astype(F32)).astype(BF16)
        return jnp.concatenate([high, low, high], axis=axis)

    def radial_part(blocks):
        rows = jnp.concatenate([block.reshape(4 * azims, radii) for block in blocks], axis=0)
        result = jnp.dot(high_low(rows, 1), radial_k[...], preferred_element_type=F32)
        rad_d[0 : len(blocks)] = result.reshape(len(blocks), 4, azims, radii)

    def azimuth_part(near, far, base, kept):
        rows = azims * az_devices if kept else azims
        for j in range(4):
            blocks = [jnp.concatenate([ref[f, base + j] for ref, f in near], axis=1)]
            for k in others:
                blocks.append(jnp.concatenate([ref[k, f, base + j] for ref, f in far], axis=1))
            column = jnp.concatenate(blocks, axis=0)
            result = jnp.dot(
                azim_k[0:rows, :], high_low(column, 0), preferred_element_type=F32
            )
            az_d[j] = result[0:azims]
            for i, f in enumerate(kept):
                for k in others:
                    far_dt[k, i, base + j] = result[
                        (k + 1) * azims : (k + 2) * azims, f * radii : (f + 1) * radii
                    ]

    def az_at(j, f):
        return az_d[j, :, f * radii : (f + 1) * radii]

    def row_of(e):
        def row(index):
            return coef[index, pl.ds(e, 1), :]

        return row

    def shot_at(step, z):
        gain = np.float32(DT * SOURCE_GAIN * math.cos(0.9 * step))
        lane = lax.broadcasted_iota(jnp.int32, (1, radii), 1)
        wanted = jnp.zeros((1, radii), jnp.int32) + source[0]
        return jnp.where((wanted == me_d * depth + z) & (lane < 4 * RB), gain, np.float32(0.0))

    def velocity_chunk(step, e):
        base = pl.multiple_of(4 * e, 4)
        planes = pl.ds(base, 4)
        row = row_of(e)
        if step == 0:
            receive_az(0, e)
        else:
            receive_az(3, e)
            for k in others:
                for j in range(4):
                    z = base + j
                    far_s[k, 1, z] = far_s[k, 1, z] + row(BM) * far_dw[k, 0, z]
                    far_s[k, 3, z] = far_s[k, 3, z] - row(PM) * far_dw[k, 0, z]
        radial_part([s_rest[0, planes], s_az[0, planes], s_rest[2, planes], s_az[3, planes]])
        azimuth_part(
            [(s_az, f) for f in range(4)], [(far_s, f) for f in range(4)], base,
            (1, 3) if step == 1 else (),
        )
        q = inv_r[...]
        for j in range(4):
            z = base + j
            rt, tt = s_az[0, z], s_az[1, z]
            rr, rz = s_rest[0, z], s_rest[2, z]
            dz = [
                dz_at(reader(ref, k), partial[f, e], base, j)
                for f, (ref, k) in enumerate(stress_dz)
            ]
            div = [
                rad_d[0, j] + q * (az_at(j, 0) + (rr - tt)) + dz[0],
                rad_d[1, j] + q * (az_at(j, 1) + 2.0 * rt) + dz[1],
                rad_d[2, j] + q * (az_at(j, 2) + rz) + dz[2],
            ]
            grad = [rad_d[3, j], q * az_at(j, 3), dz[3]]
            solid = [(v_az, 0), (v_az, 2), (v_az, 1)]
            fluid = [(v_rest, 0), (v_az, 3), (v_rest, 1)]
            for c in range(3):
                psi = [mem[3 * pole + c, z] for pole in range(4)]
                resist = grad[c]
                for pole in range(4):
                    resist = resist + row(FA + pole) * psi[pole]
                ref, k = solid[c]
                ref[k, z] = ref[k, z] + (row(A1) * div[c] + row(A2) * resist)
                change = -(row(A2) * div[c] + row(A3) * resist)
                ref, k = fluid[c]
                fresh = ref[k, z] + change
                ref[k, z] = fresh
                change = change + row(OM) * fresh
                psi = [(psi[pole] + change) * row(INV + pole) for pole in range(4)]
                for pole in range(4):
                    mem[3 * pole + c, z] = psi[pole]
                if c == 1 and step == 0:
                    total = row(FA) * psi[0]
                    for pole in range(1, 4):
                        total = total + row(FA + pole) * psi[pole]
                    psi_t[0, z] = total

    def stress_chunk(step, e):
        base = pl.multiple_of(4 * e, 4)
        planes = pl.ds(base, 4)
        radial_part([v_az[0, planes], v_az[2, planes], v_az[1, planes], v_rest[0, planes]])
        if step == 0:
            receive_az(1, e)
            far = [(far_v, f) for f in range(4)]
        else:
            receive_az(4, e)
            far = [(far_new, 0), (far_new, 1), (far_v, 2), (far_v, 3)]
        azimuth_part([(v_az, f) for f in range(4)], far, base, (0, 1, 2) if step == 0 else ())
        row = row_of(e)
        q = inv_r[...]
        for j in range(4):
            z = base + j
            vr, vt, wr = v_az[0, z], v_az[2, z], v_rest[0, z]
            dz = [
                dz_at(reader(ref, k), partial[f, e], base, j)
                for f, (ref, k) in enumerate(vel_dz)
            ]
            e_rr = rad_d[0, j]
            e_tt = q * (vr + az_at(j, 2))
            e_zz = dz[1]
            g_rt = q * (az_at(j, 0) - vt) + rad_d[1, j]
            g_rz = dz[0] + rad_d[2, j]
            g_tz = dz[2] + q * az_at(j, 1)
            div_v = e_rr + e_tt + e_zz
            div_w = rad_d[3, j] + q * (wr + az_at(j, 3)) + dz[3]
            if step == 0:
                dw[0, z] = div_w
            bulk = row(LF) * div_v + row(BM) * div_w
            twice = 2.0 * row(MU)
            s_rest[0, z] = s_rest[0, z] + (bulk + twice * e_rr)
            s_az[1, z] = s_az[1, z] + (bulk + twice * e_tt)
            s_rest[1, z] = s_rest[1, z] + (bulk + twice * e_zz)
            s_az[0, z] = s_az[0, z] + row(MU) * g_rt
            s_rest[2, z] = s_rest[2, z] + row(MU) * g_rz
            s_az[2, z] = s_az[2, z] + row(MU) * g_tz
            s_az[3, z] = s_az[3, z] - (row(BM) * div_v + row(PM) * div_w) + shot_at(step, z)

    def far_stress_chunk(e):
        base = pl.multiple_of(4 * e, 4)
        planes = pl.ds(base, 4)
        row = row_of(e)
        q = inv_r[...]
        for k in others:
            radial_part([far_v[k, 0, planes], far_v[k, 2, planes]])
            for j in range(4):
                z = base + j
                vr, vt = far_v[k, 0, z], far_v[k, 2, z]
                dz_vz = dz_at(far_reader(far_v, k, 1), far_partial[k, 0, e], base, j)
                dz_vt = dz_at(far_reader(far_v, k, 2), far_partial[k, 1, e], base, j)
                e_tt = q * (vr + far_dt[k, 2, z])
                div_v = rad_d[0, j] + e_tt + dz_vz
                g_rt = q * (far_dt[k, 0, z] - vt) + rad_d[1, j]
                g_tz = dz_vt + q * far_dt[k, 1, z]
                far_s[k, 0, z] = far_s[k, 0, z] + row(MU) * g_rt
                far_s[k, 1, z] = far_s[k, 1, z] + (row(LF) * div_v + 2.0 * row(MU) * e_tt)
                far_s[k, 2, z] = far_s[k, 2, z] + row(MU) * g_tz
                far_s[k, 3, z] = far_s[k, 3, z] - row(BM) * div_v + shot_at(0, z)

    def far_velocity_chunk(e):
        base = pl.multiple_of(4 * e, 4)
        planes = pl.ds(base, 4)
        row = row_of(e)
        q = inv_r[...]
        receive_az(2, e)
        for k in others:
            radial_part([far_s[k, 0, planes]])
            for j in range(4):
                z = base + j
                dz_tz = dz_at(far_reader(far_s, k, 2), far_partial[k, 0, e], base, j)
                div = rad_d[0, j] + q * (far_dt[k, 0, z] + 2.0 * far_s[k, 0, z]) + dz_tz
                resist = q * far_dt[k, 1, z] + far_psi[k, 0, z]
                far_v[k, 2, z] = far_v[k, 2, z] + (row(A1) * div + row(A2) * resist)
                far_v[k, 3, z] = far_v[k, 3, z] - (row(A2) * div + row(A3) * resist)

    def each_chunk(body):
        def wrapped(e, carry):
            body(e)
            return carry

        lax.fori_loop(0, chunks, wrapped, 0)

    for e in order:
        for copy in first_loads(e):
            copy.wait()
        start_az(0, e)
    for index in (0, 2, 4):
        loads[index].wait()
    send_down(0, stress_dz)
    send_up(0, stress_dz)
    for index in range(14, 19):
        loads[index].wait()

    elements = ids.shape[1]
    spread = lax.broadcasted_iota(jnp.int32, (elements, radii), 0) == (
        lax.broadcasted_iota(jnp.int32, (elements, radii), 1) >> 2
    )
    ids_node = jnp.dot(
        ids[...].astype(F32).astype(BF16), spread.astype(F32).astype(BF16),
        preferred_element_type=F32,
    )
    node = lax.broadcasted_iota(jnp.int32, (1, radii), 1)
    place = node & 3
    inside = jnp.zeros((1, radii), F32)
    for j in range(1, 4):
        inside = jnp.where(place == j, np.float32(0.5 * (1.0 + gll_nodes[j])), inside)
    inv_r[...] = 1.0 / (np.float32(R_INNER) + (node >> 2).astype(F32) + inside)

    def pick(table, column):
        value = jnp.zeros_like(ids_node)
        for r in range(8):
            value = jnp.where(ids_node == float(r), table[r : r + 1, column : column + 1], value)
        return value

    lame_zero, shear, modulus, coupling, rho, rho_f, tort, fric = [pick(mats, c) for c in range(8)]
    omega = pick(jkd, 0)
    rho_w = rho_f * tort
    scale = DT / (rho * rho_w - rho_f * rho_f)
    coef[A1] = rho_w * scale
    coef[A2] = rho_f * scale
    coef[A3] = rho * scale
    for pole in range(4):
        coef[FA + pole] = fric * pick(jkd, 1 + pole)
        coef[INV + pole] = 1.0 / (1.0 + DT * (pick(jkd, 5 + pole) + omega))
    coef[OM] = DT * omega
    coef[LF] = DT * (lame_zero + coupling * coupling * modulus)
    coef[BM] = DT * coupling * modulus
    coef[MU] = DT * shear
    coef[PM] = DT * modulus

    for index in range(7, 14):
        loads[index].wait()

    stores = []

    def to_out(src, dst):
        copy = pltpu.make_async_copy(src, dst, store_sem.at[len(stores)])
        copy.start()
        stores.append(copy)

    receive_halos(0, stress_dz)

    def first_velocity(turn):
        last = chunks - 1
        e = jnp.where(turn == 0, 0, jnp.where(turn == 1, last, turn - 1))
        velocity_chunk(0, e)

        @pl.when(turn == 0)
        def _():
            send_down(1, vel_dz)

        @pl.when(turn == min(1, last))
        def _():
            send_up(1, vel_dz)

        @pl.when((turn != 1) | (last == 1))
        def _():
            start_az(1, e)

        @pl.when((turn == last) & (last > 1))
        def _():
            start_az(1, last)

    each_chunk(first_velocity)
    for e in range(chunks):
        start_az(2, e)
    finish_az(0)
    finish_halos(0)

    receive_halos(1, vel_dz)

    def first_stress(e):
        stress_chunk(0, e)
        start_az(3, e)

        @pl.when(e == 0)
        def _():
            send_down(2, stress_dz)

        @pl.when(e == chunks - 1)
        def _():
            send_up(2, stress_dz)
            receive_far_top(1, far_v)

        @pl.when(e == 1)
        def _():
            receive_far_bottom(1, far_v)

        @pl.when(e > 0)
        def _():
            far_partials(1, far_v, e)
            far_stress_chunk(e - 1)

    each_chunk(first_stress)
    far_stress_chunk(chunks - 1)
    finish_az(1)
    finish_halos(1)

    receive_halos(2, stress_dz)

    def second_velocity(e):
        velocity_chunk(1, e)
        start_az(4, e)

        @pl.when(e == 0)
        def _():
            send_down(3, vel_dz)

    each_chunk(second_velocity)
    send_up(3, vel_dz)
    for i, (ref, k) in enumerate(vel_place):
        to_out(ref.at[k, inner], vel_out.at[i])
    to_out(mem, mem_out)
    receive_far_top(2, far_s)
    receive_far_bottom(2, far_s)
    for e in range(1, chunks):
        far_partials(2, far_s, e)
    each_chunk(far_velocity_chunk)
    finish_az(2)
    finish_az(3)
    finish_halos(2)

    receive_halos(3, vel_dz)

    def chunk_stores(e):
        planes = pl.ds(pl.multiple_of(4 * e, 4), 4)
        return [
            pltpu.make_async_copy(ref.at[k, planes], str_out.at[i, planes], chunk_sem.at[e, i])
            for i, (ref, k) in enumerate(stress_place)
        ]

    def second_stress(e):
        stress_chunk(1, e)
        for copy in chunk_stores(e):
            copy.start()

    each_chunk(second_stress)
    finish_az(4)
    finish_halos(3)
    for copy in stores:
        copy.wait()
    for e in range(chunks):
        for copy in chunk_stores(e):
            copy.wait()


FAR_DZ = {1: (1, 2), 2: (2,)}


def deliver_kernel(vel_in, str_in, mem_in, vel_out, str_out, mem_out, held, load_sem, store_sem):
    rows = [(src.at[i], dst.at[i]) for src, dst in ((mem_in, mem_out), (str_in, str_out), (vel_in, vel_out))
            for i in range(src.shape[0])]
    loads = [
        pltpu.make_async_copy(src, held.at[i], load_sem.at[i]) for i, (src, dst) in enumerate(rows)
    ]
    stores = [
        pltpu.make_async_copy(held.at[i], dst, store_sem.at[i]) for i, (src, dst) in enumerate(rows)
    ]
    for copy in loads:
        copy.start()
    for load, store in zip(loads, stores):
        load.wait()
        store.start()
    for copy in stores:
        copy.wait()


def on_device(depth_devices, az_devices, velocity, stress, memory, layer_ids, materials, jkd, source_depth):
    depth, azims, radii = velocity.shape[1:]
    chunks = depth // 4
    halves = 2 * STEPS
    others = max(az_devices - 1, 1)
    azim_total = azims * az_devices
    radial_high, radial_low = split_high_low(radial_operator(radii).T)
    radial_k = np.concatenate([radial_high, radial_high, radial_low], axis=0)
    azim_high, azim_low = split_high_low(azimuth_operator(azim_total))
    azim_k = np.concatenate([azim_high, azim_high, azim_low], axis=1)
    plane = (azims, radii)
    smem = pl.BlockSpec(memory_space=pltpu.SMEM)
    hbm = pl.BlockSpec(memory_space=pltpu.HBM)
    dma = pltpu.SemaphoreType.DMA
    constants = [radial_k, azim_k]
    small = [materials, jkd, layer_ids] + [jnp.asarray(value) for value in constants]

    def held(*shape):
        return pltpu.VMEM(shape + plane, F32)

    results = pl.pallas_call(
        functools.partial(step_kernel, depth_devices, az_devices),
        out_shape=tuple(jax.ShapeDtypeStruct(x.shape, x.dtype) for x in (velocity, stress, memory)),
        in_specs=[smem] + [hbm] * 8,
        out_specs=(hbm, hbm, hbm),
        scratch_shapes=[pltpu.VMEM(value.shape, value.dtype) for value in small] + [
            held(12, depth),
            pltpu.VMEM((1, radii), F32),
            held(4, depth + 1),
            held(3, depth + 1),
            held(4, depth + 1),
            held(2, depth + 1),
            held(others, 4, depth + 1),
            held(others, 4, depth + 1),
            held(others, 2, depth),
            held(others, 1, depth),
            held(others, 1, depth),
            held(others, 3, depth),
            held(1, depth),
            held(1, depth),
            held(halves, 4),
            held(halves, 4),
            held(2, others, 2),
            held(2, others, 2),
            held(halves, 4),
            held(halves, 4),
            held(4, chunks),
            held(others, 2, chunks),
            pltpu.VMEM((NCOEF, chunks, radii), F32),
            held(4, 4),
            pltpu.VMEM((4, azims, 4 * radii), F32),
            dma((19,)),
            dma((chunks, 4)),
            dma((7,)),
            dma((chunks, 7)),
            dma((5, others, chunks)),
            dma((5, others, chunks)),
            dma((halves, others + 1)),
            dma((halves, others + 1)),
            dma((halves, others + 1)),
            dma((halves, others + 1)),
        ],
        compiler_params=pltpu.CompilerParams(
            collective_id=0, has_side_effects=True, vmem_limit_bytes=64 * 1024 * 1024
        ),
        cost_estimate=pl.CostEstimate(
            flops=10**9, bytes_accessed=2 * 25 * velocity.size // 6 * 4, transcendentals=0
        ),
        name="biot_steps",
    )(source_depth, *small, velocity, stress, memory)
    return tuple(pl.pallas_call(
        deliver_kernel,
        out_shape=tuple(jax.ShapeDtypeStruct(x.shape, x.dtype) for x in results),
        in_specs=[hbm] * 3,
        out_specs=(hbm,) * 3,
        scratch_shapes=[held(25, depth), dma((25,)), dma((25,))],
        compiler_params=pltpu.CompilerParams(vmem_limit_bytes=64 * 1024 * 1024),
        cost_estimate=pl.CostEstimate(
            flops=0, bytes_accessed=2 * 25 * velocity.size // 6 * 4, transcendentals=0
        ),
        name="deliver",
    )(*results))


def solution(mesh):
    return jax.shard_map(
        functools.partial(on_device, mesh.shape["depth"], mesh.shape["az"]),
        mesh=mesh,
        in_specs=(
            P(None, "depth", "az", None),
            P(None, "depth", "az", None),
            P(None, "depth", "az", None),
            P("depth", None),
            P(),
            P(),
            P(),
        ),
        out_specs=(
            P(None, "depth", "az", None),
            P(None, "depth", "az", None),
            P(None, "depth", "az", None),
        ),
        check_vma=False,
    )
```
